128 devices in a mesh: col: 16 (over y, z), dp: 4 (over x_lo, core), strip: 2 (over x_hi).
Axes of the slice: x: 4 (x_hi: 2, x_lo: 2; x = x_hi * 2 + x_lo), y: 4, z: 4, core: 2. Of those that a mesh axis runs over, the one named last changes fastest.
Arguments:
- stem: bfloat16 [16, 4, 32, 360], P('dp', 'strip'), may hold values from -6 to 6
- labels: int32 [16, 4, 32], P('dp', 'strip'), may hold values from 0 to 149
- up_proj: bfloat16 [16, 720, 360], P('col'), may hold values from -0.21875 to 0.21875
- mix_proj: bfloat16 [16, 360, 360], P('col'), may hold values from -0.3125 to 0.3125
- down_proj: bfloat16 [16, 360, 720], P('col'), may hold values from -0.3125 to 0.3125
- dw_kernel: bfloat16 [16, 9, 360], P('col'), may hold values from -2 to 2
- gain1: float32 [16, 360], P('col'), may hold values from 0.7498942 to 1
- gain2: float32 [16, 720], P('col'), may hold values from 0.7498942 to 1
- lat_one: bfloat16 [360, 512], replicated, may hold values from -0.3125 to 0.3125
- lat_two: bfloat16 [720, 512], replicated, may hold values from -0.21875 to 0.21875
- classifier: bfloat16 [512, 150], replicated, may hold values from -1.0546875 to 1.0546875
Outputs:
- grad_up: float32 [16, 720, 360], P('col', ('dp', 'strip'))
- grad_mix: float32 [16, 360, 360], P('col', ('dp', 'strip'))
- grad_down: float32 [16, 360, 720], P('col', ('dp', 'strip'))
- grad_kernel: float32 [16, 9, 360], P('col', None, ('dp', 'strip'))
- grad_stem: float32 [16, 4, 32, 360], P('dp', 'strip', 'col')
The draws below stay inside these ranges and needn't reach their ends.
All inputs are finite; a program needn't handle non-finite values.
Results may differ from the reference program's by a relative error of at most 0.034.
Values sent between devices are 32-bit elements; how exact they have to be, the bound alone decides.
No kernel may reach another device: no remote copies, remote signals or barrier semaphores. Data moves between devices by JAX's collectives and lax.ppermute only.
A program may use at most 64 MiB of HBM per device.

```python
import math
import jax
import jax.numpy as jnp
from jax import lax

C1 = 360
C2 = 720
HEAD = 512
CLASSES = 150
W1 = 32
COLS = 16
BATCH = 16
H1 = 4


def plant(values, own_key, smallest, largest):
    longest = values.shape.index(max(values.shape))
    spots = []
    for shift in (0, 1):
        where = [jax.random.randint(jax.random.fold_in(own_key, axis), (), 0, length) for axis, length in enumerate(values.shape)]
        where[longest] = (where[longest] + shift) % values.shape[longest]
        spots.append(tuple(where))
    return values.at[spots[0]].set(smallest).at[spots[1]].set(largest)


def shard_levels(own_key, shape, cuts, low, top_value):
    def one(axis_at, parts):
        steps = jax.random.uniform(jax.random.fold_in(jax.random.fold_in(own_key, 6), axis_at), (parts,), jnp.float32, low / len(cuts), top_value / len(cuts))
        return jnp.repeat(jnp.exp(steps), shape[axis_at] // parts).reshape((-1,) + (1,) * (len(shape) - axis_at - 1))

    level = one(*cuts[0])
    for cut in cuts[1:]:
        level = level * one(*cut)
    return level


def noise(own_key, dims, scale, limit, cuts=(), kind=jnp.bfloat16):
    values = jax.random.normal(own_key, dims, jnp.float32) * scale
    if len(cuts) > 0:
        values = shard_levels(own_key, dims, cuts, -0.22, 0.18) * values
    return jnp.clip(values, min=-limit, max=limit).astype(kind)


def setup_inputs(seed: int = 0) -> dict:
    arg_keys = jax.random.split(jax.random.key(seed), 12)
    return {
        "stem": noise(arg_keys[0], (BATCH, H1, W1, C1), 1.0, 6.0, ((0, 4), (1, 2))),
        "labels": plant(jax.random.randint(arg_keys[1], (BATCH, H1, W1), 0, CLASSES), jax.random.fold_in(arg_keys[1], 1), 0, CLASSES - 1).astype(jnp.int32),
        "up_proj": noise(arg_keys[2], (COLS, C2, C1), C2 ** -0.5, 0.21875, ((0, 16),)),
        "mix_proj": noise(arg_keys[3], (COLS, C1, C1), C1 ** -0.5, 0.3125, ((0, 16),)),
        "down_proj": noise(arg_keys[4], (COLS, C1, C2), C1 ** -0.5, 0.3125, ((0, 16),)),
        "dw_kernel": noise(arg_keys[5], (COLS, 9, C1), 9 ** -0.5, 2.0, ((0, 16),)),
        "gain1": jnp.clip(jnp.exp(math.log(1.0) - 0.28782315 * jax.random.uniform(arg_keys[6], (COLS, C1), jnp.float32) ** shard_levels(arg_keys[6], (COLS, C1), ((0, 16),), -0.2, 0.2)), 0.7498942, 1.0),
        "gain2": jnp.clip(jnp.exp(math.log(1.0) - 0.28782315 * jax.random.uniform(arg_keys[7], (COLS, C2), jnp.float32) ** shard_levels(arg_keys[7], (COLS, C2), ((0, 16),), -0.2, 0.2)), 0.7498942, 1.0),
        "lat_one": noise(arg_keys[8], (C1, HEAD), C1 ** -0.5, 0.3125),
        "lat_two": noise(arg_keys[9], (C2, HEAD), C2 ** -0.5, 0.21875),
        "classifier": noise(arg_keys[10], (HEAD, CLASSES), (4.0 / HEAD ** 0.5), 1.0546875),
    }


loss_scale = 64.0
root_coef = 0.7978845608028654
cube_coef = 0.044715


def gelu_pair(values):
    inner = root_coef * (values + cube_coef * values * values * values)
    tangent = jnp.tanh(inner)
    result = 0.5 * values * (1.0 + tangent)
    slope = 0.5 * (1.0 + tangent) + 0.5 * values * (1.0 - tangent * tangent) * root_coef * (1.0 + 3.0 * cube_coef * values * values)
    return result, slope


def project(left, matrix):
    flat = left.reshape(-1, left.shape[-1])
    out = jnp.dot(flat, matrix, preferred_element_type=jnp.float32)
    return out.reshape(left.shape[:-1] + (matrix.shape[1],))


def project_back(left, matrix):
    flat = left.reshape(-1, left.shape[-1])
    out = lax.dot_general(flat, matrix, (((1,), (1,)), ((), ())), preferred_element_type=jnp.float32)
    return out.reshape(left.shape[:-1] + (matrix.shape[0],))


def outer_sum(left, right):
    return lax.dot_general(left.reshape(-1, left.shape[-1]), right.reshape(-1, right.shape[-1]), (((0,), (0,)), ((), ())), preferred_element_type=jnp.float32)


def upsample(values):
    return jnp.repeat(jnp.repeat(values, 2, axis=-3), 2, axis=-2)


def pool_sum(values):
    shape = values.shape
    return values.reshape(shape[:-3] + (shape[-3] // 2, 2, shape[-2] // 2, 2, shape[-1])).sum(axis=(-4, -2))


def depthwise_apply(padded, kernel):
    row_count = padded.shape[-3] - 2
    col_count = padded.shape[-2] - 2
    total = jnp.zeros(padded.shape[:-3] + (row_count, col_count, padded.shape[-1]), jnp.float32)
    for tap_index in range(9):
        row_shift = tap_index // 3 - 1
        col_shift = tap_index % 3 - 1
        total = total + kernel[tap_index] * padded[..., 1 + row_shift:1 + row_shift + row_count, 1 + col_shift:1 + col_shift + col_count, :]
    return total


def depthwise_adjoint(padded, kernel):
    row_count = padded.shape[-3] - 2
    col_count = padded.shape[-2] - 2
    total = jnp.zeros(padded.shape[:-3] + (row_count, col_count, padded.shape[-1]), jnp.float32)
    for tap_index in range(9):
        row_shift = tap_index // 3 - 1
        col_shift = tap_index % 3 - 1
        total = total + kernel[tap_index] * padded[..., 1 - row_shift:1 - row_shift + row_count, 1 - col_shift:1 - col_shift + col_count, :]
    return total


def kernel_terms(padded, grad_depth):
    row_count = grad_depth.shape[-3]
    col_count = grad_depth.shape[-2]
    axes = tuple(range(grad_depth.ndim - 1))
    pieces = []
    for tap_index in range(9):
        row_shift = tap_index // 3 - 1
        col_shift = tap_index % 3 - 1
        window = padded[..., 1 + row_shift:1 + row_shift + row_count, 1 + col_shift:1 + col_shift + col_count, :]
        pieces.append(jnp.sum(window * grad_depth, axis=axes))
    return jnp.stack(pieces, axis=0)


def head_grads(level_one, level_two, lat_one, lat_two, classifier, labels, npix):
    lateral = project(level_one.astype(jnp.bfloat16), lat_one) + upsample(project(level_two.astype(jnp.bfloat16), lat_two))
    active, slope = gelu_pair(lateral)
    hidden = active.astype(jnp.bfloat16)
    logits = project(hidden, classifier)
    probs = jax.nn.softmax(logits, axis=-1)
    onehot = (labels[..., None] == jnp.arange(classifier.shape[1], dtype=jnp.int32)).astype(jnp.float32)
    grad_logits = (probs - onehot) * (loss_scale / npix)
    grad_lat = project_back(grad_logits.astype(jnp.bfloat16), classifier) * slope
    cot_one = project_back(grad_lat.astype(jnp.bfloat16), lat_one)
    cot_two = project_back(pool_sum(grad_lat).astype(jnp.bfloat16), lat_two)
    return cot_one, cot_two


def pad_crop(values):
    return jnp.pad(values, ((0, 0), (1, 1), (1, 1), (0, 0)))


def reference(stem, labels, up_proj, mix_proj, down_proj, dw_kernel, gain1, gain2, lat_one, lat_two, classifier):
    columns = up_proj.shape[0]
    crops, height, width, chan_one = stem.shape
    chan_two = up_proj.shape[1]
    state_one = jnp.zeros((crops, height, width, chan_one), jnp.float32)
    state_two = jnp.zeros((crops, height // 2, width // 2, chan_two), jnp.float32)
    stem_wide = stem.astype(jnp.float32)
    saves = []
    for column in range(columns):
        kernel = dw_kernel[column].astype(jnp.float32)
        narrow = state_two.astype(jnp.bfloat16)
        mixture = stem_wide + upsample(project(narrow, up_proj[column]))
        padded = pad_crop(mixture)
        depth = depthwise_apply(padded, kernel)
        active, slope_one = gelu_pair(depth)
        hidden = active.astype(jnp.bfloat16)
        state_one = gain1[column] * state_one + project(hidden, mix_proj[column])
        pooled = (pool_sum(state_one) * 0.25).astype(jnp.bfloat16)
        lifted, slope_two = gelu_pair(project(pooled, down_proj[column]))
        state_two = gain2[column] * state_two + lifted
        saves.append((narrow, padded, slope_one, hidden, pooled, slope_two))
    npix = float(crops * height * width)
    cot_one, cot_two = head_grads(state_one, state_two, lat_one, lat_two, classifier, labels, npix)
    grads_up = [None] * columns
    grads_mix = [None] * columns
    grads_down = [None] * columns
    grads_kernel = [None] * columns
    grad_stem = jnp.zeros(stem.shape, jnp.float32)
    for column in range(columns - 1, -1, -1):
        narrow, padded, slope_one, hidden, pooled, slope_two = saves[column]
        kernel = dw_kernel[column].astype(jnp.float32)
        grad_lift = (cot_two * slope_two).astype(jnp.bfloat16)
        grads_down[column] = outer_sum(pooled, grad_lift)
        total_one = cot_one + upsample(project_back(grad_lift, down_proj[column])) * 0.25
        total_narrow = total_one.astype(jnp.bfloat16)
        grads_mix[column] = outer_sum(hidden, total_narrow)
        grad_depth = project_back(total_narrow, mix_proj[column]) * slope_one
        grads_kernel[column] = kernel_terms(padded, grad_depth)
        grad_mixture = depthwise_adjoint(pad_crop(grad_depth), kernel)
        grad_stem = grad_stem + grad_mixture
        grad_narrow = pool_sum(grad_mixture).astype(jnp.bfloat16)
        grads_up[column] = outer_sum(narrow, grad_narrow)
        cot_two = gain2[column] * cot_two + project_back(grad_narrow, up_proj[column])
        cot_one = gain1[column] * total_one
    return (jnp.stack(grads_up, 0), jnp.stack(grads_mix, 0), jnp.stack(grads_down, 0), jnp.stack(grads_kernel, 0), grad_stem)
```

```python
import jax
import jax.numpy as jnp
from jax import lax
from jax.experimental import pallas as pl
from jax.experimental.pallas import tpu as pltpu
from jax.sharding import Mesh, PartitionSpec as P

loss_scale = 64.0
root_coef = 0.7978845608028654
cube_coef = 0.044715

C1 = 360
C2 = 720
PAD1 = 384
HEAD = 512
CLASSES = 150
F32 = jnp.float32
BF16 = jnp.bfloat16
VMEM_LIMIT = 30 * 2**20

WROWS = 464
LROWS = 224
RROWS = 240
GROWS = 256


def params():
    return pltpu.CompilerParams(vmem_limit_bytes=VMEM_LIMIT)


def gelu_pair(values):
    inner = root_coef * (values + cube_coef * values * values * values)
    tangent = jnp.tanh(inner)
    result = 0.5 * values * (1.0 + tangent)
    slope = 0.5 * (1.0 + tangent) + 0.5 * values * (1.0 - tangent * tangent) * root_coef * (
        1.0 + 3.0 * cube_coef * values * values
    )
    return result, slope


def gelu_only(values):
    inner = root_coef * (values + cube_coef * values * values * values)
    return 0.5 * values * (1.0 + jnp.tanh(inner))


def dot(left, right):
    return jnp.dot(left, right, preferred_element_type=F32)


def dot_nt(left, right):
    return lax.dot_general(left, right, (((1,), (1,)), ((), ())), preferred_element_type=F32)


def dot_tn(left, right):
    return lax.dot_general(left, right, (((0,), (0,)), ((), ())), preferred_element_type=F32)


def shifted(even, odd):
    spot = lax.broadcasted_iota(jnp.int32, even.shape, 0)
    after = jnp.where(spot == 15, 0.0, pltpu.roll(even, 15, 0))
    before = jnp.where(spot == 0, 0.0, pltpu.roll(odd, 1, 0))
    return after, before


def neighbours(blocks):
    rows = []
    for r in range(4):
        even, odd = blocks[2 * r], blocks[2 * r + 1]
        after, before = shifted(even, odd)
        rows.append(((before, even, odd), (even, odd, after)))
    return rows


def stencil(rows, taps):
    out = []
    for r in range(4):
        for b in range(2):
            total = None
            for i in (-1, 0, 1):
                if 0 <= r + i < 4:
                    for j in range(3):
                        term = taps[3 * (i + 1) + j] * rows[r + i][b][j]
                        total = term if total is None else total + term
            out.append(total)
    return out


def tap_sums(rows, grads):
    sums = []
    for i in (-1, 0, 1):
        for j in range(3):
            total = None
            for r in range(4):
                if 0 <= r + i < 4:
                    for b in range(2):
                        term = rows[r + i][b][j] * grads[2 * r + b]
                        total = term if total is None else total + term
            sums.append(jnp.sum(total, axis=0, keepdims=True))
    return sums


def pool(blocks):
    parts = [blocks[4 * q] + blocks[4 * q + 1] + blocks[4 * q + 2] + blocks[4 * q + 3] for q in range(2)]
    return jnp.concatenate(parts, axis=0)


def split(values):
    return [values[16 * q : 16 * q + 16] for q in range(8)]


def join(blocks):
    return jnp.concatenate(blocks, axis=0)


def up2(values):
    return [values[16 * (q // 4) : 16 * (q // 4) + 16] for q in range(8)]


def decode_aux(aux):
    taps = [aux[t : t + 1, 0:C1] for t in range(8)] + [aux[0:1, PAD1 : PAD1 + C1]]
    gain1 = aux[1:2, PAD1 : PAD1 + C1]
    gain2 = jnp.concatenate([aux[2:3, PAD1 : 2 * PAD1], aux[3:4, PAD1:C2]], axis=1)
    return taps, gain1, gain2


def put(ref, row, values):
    width = values.shape[1]
    if width < PAD1:
        values = jnp.concatenate([values, jnp.zeros((values.shape[0], PAD1 - width), F32)], axis=1)
    ref[row : row + values.shape[0], :] = values


def put_two(ref, row, values):
    put(ref, row, values[:, 0:PAD1])
    put(ref, row + values.shape[0], values[:, PAD1:C2])


def get_two(ref, row):
    return jnp.concatenate([ref[row : row + 32, :], ref[row + 32 : row + 64, 0 : C2 - PAD1]], axis=1)


def pack_kernel(where, up_ref, mix_ref, down_ref, tap_ref, g1_ref, g2_ref, out_ref):
    core = where[2]
    mix = mix_ref[0].astype(F32)

    @pl.when(core == 0)
    def _():
        up = up_ref[0].astype(F32)
        out_ref[0:368, 0:C1] = up[0:368]
        out_ref[0:352, PAD1 : PAD1 + C1] = up[368:720]
        out_ref[368:464, 0:C1] = mix[0:96]
        out_ref[368:464, PAD1 : PAD1 + C1] = mix[96:192]

    @pl.when(core == 1)
    def _():
        down = down_ref[0].astype(F32)
        taps = tap_ref[0].astype(F32)
        out_ref[0:360, 0:C2] = down
        out_ref[360:368, 0:C1] = taps[0:8]
        out_ref[360:361, PAD1 : PAD1 + C1] = taps[8:9]
        out_ref[361:362, PAD1 : PAD1 + C1] = g1_ref[...]
        out_ref[362:363, PAD1 : 2 * PAD1] = g2_ref[:, 0:PAD1]
        out_ref[363:364, PAD1:C2] = g2_ref[:, PAD1:C2]
        out_ref[368:464, 0:C1] = mix[192:288]
        out_ref[368:440, PAD1 : PAD1 + C1] = mix[288:360]


def unpack_kernel(where, o0, o1, r1, r2, r3, s1, s2, s3, up_ref, mix_ref, down_ref, aux_ref):
    z, core = where[1], where[2]

    def write(first, second, column):
        up = jnp.concatenate([first[0:368, 0:C1], first[0:352, PAD1 : PAD1 + C1]], axis=0)
        up_ref[column] = up.astype(BF16)
        mix = jnp.concatenate(
            [
                first[368:464, 0:C1],
                first[368:464, PAD1 : PAD1 + C1],
                second[368:464, 0:C1],
                second[368:440, PAD1 : PAD1 + C1],
            ],
            axis=0,
        )
        mix_ref[column] = mix.astype(BF16)
        down_ref[column] = second[0:360, 0:C2].astype(BF16)
        aux_ref[column] = second[360:368, :]

    last, following, opposite = lax.rem(z + 3, 4), lax.rem(z + 1, 4), lax.rem(z + 2, 4)

    @pl.when(core == 0)
    def _():
        write(o0, o1, z)
        write(r1, s2, last)
        write(r2, s1, following)
        write(r3, s3, opposite)

    @pl.when(core == 1)
    def _():
        write(o1, o0, z)
        write(s1, r2, last)
        write(s2, r1, following)
        write(s3, r3, opposite)


def forward_kernel(full, where, msg_ref, stem_ref, up_ref, mix_ref, down_ref, aux_ref, out_ref, *rest):
    if full:
        mixture_ref, slope1_ref, slope2_ref, left_ref, half_ref, state1, state2 = rest
    else:
        state1, state2 = rest
    step = pl.program_id(0)

    @pl.when(step == 0)
    def _():
        state1[...] = msg_ref[0:128, 0:C1]
        state2[...] = get_two(msg_ref, 128)

    taps, gain1, gain2 = decode_aux(aux_ref[0])
    narrow = state2[...].astype(BF16)
    lifted_up = dot(narrow, up_ref[0])
    ups = up2(lifted_up)
    mixture = [stem_ref[16 * q : 16 * q + 16, 0:C1] + ups[q] for q in range(8)]
    depth = join(stencil(neighbours(mixture), taps))
    if full:
        active, slope1 = gelu_pair(depth)
    else:
        active = gelu_only(depth)
    hidden = active.astype(BF16)
    next1 = gain1 * state1[...] + dot(hidden, mix_ref[0])
    pooled = (pool(split(next1)) * 0.25).astype(BF16)
    lifted = dot(pooled, down_ref[0])
    if full:
        active2, slope2 = gelu_pair(lifted)
    else:
        active2 = gelu_only(lifted)
    next2 = gain2 * state2[...] + active2
    state1[...] = next1
    state2[...] = next2
    if full:
        core = where[2]
        mixture_ref[0] = join(mixture)
        slope1_ref[0] = slope1
        slope2_ref[0] = slope2
        here = left_ref.at[0]
        put(here, 0, hidden.astype(F32))
        put(here, 128, pooled.astype(F32))
        put_two(here, 160, narrow.astype(F32))
        half = LROWS // 2
        half_ref[0] = left_ref[0, pl.ds(pl.multiple_of(core * half, 8), half), :]

    @pl.when(step == 3)
    def _():
        put(out_ref, 0, next1)
        put_two(out_ref, 128, next2)


def head_kernel(where, msg_ref, stem_ref, one_ref, two_ref, cls_ref, out_ref, first, second):
    state1 = msg_ref[0:128, 0:C1].astype(BF16)
    state2 = get_two(msg_ref, 128).astype(BF16)
    labels = stem_ref[:, C1 : C1 + 1].astype(jnp.int32)
    second[...] = dot(state2, two_ref[...])
    first[...] = dot(state1, one_ref[...])
    lateral = first[...] + join(up2(second[...]))
    active, slope = gelu_pair(lateral)
    logits = dot(active.astype(BF16), cls_ref[...])
    classes = lax.broadcasted_iota(jnp.int32, logits.shape, 1)
    logits = jnp.where(classes < CLASSES, logits, -jnp.inf)
    logits = logits - jnp.max(logits, axis=-1, keepdims=True)
    powers = jnp.exp(logits)
    probs = powers / jnp.sum(powers, axis=-1, keepdims=True)
    onehot = (classes == labels).astype(F32)
    grad_logits = (probs - onehot) * (loss_scale / 2048.0)
    grad_lat = dot_nt(grad_logits.astype(BF16), cls_ref[...]) * slope
    put(out_ref, 0, dot_nt(grad_lat.astype(BF16), one_ref[...]))
    put_two(out_ref, 128, dot_nt(pool(split(grad_lat)).astype(BF16), two_ref[...]))


def backward_kernel(
    full, where, msg_ref, head_ref, slope1_ref, slope2_ref, up_ref, mix_ref, down_ref, aux_ref, *rest
):
    if full:
        mixture_ref, out_ref, right_ref, half_ref, stem_out, cot1, cot2, stem_sum = rest
    else:
        out_ref, cot1, cot2 = rest
    step = pl.program_id(0)

    @pl.when(step == 0)
    def _():
        @pl.when(where[0] == 3)
        def _():
            cot1[...] = head_ref[0:128, 0:C1]
            cot2[...] = get_two(head_ref, 128)

        @pl.when(where[0] != 3)
        def _():
            cot1[...] = msg_ref[0:128, 0:C1]
            cot2[...] = get_two(msg_ref, 128)

    taps, gain1, gain2 = decode_aux(aux_ref[0])
    old2 = cot2[...]
    grad_s = (old2 * slope2_ref[0]).astype(BF16)
    back = dot_nt(grad_s, down_ref[0]) * 0.25
    total1 = cot1[...] + join(up2(back))
    narrow_total = total1.astype(BF16)
    grad_depth = dot_nt(narrow_total, mix_ref[0]) * slope1_ref[0]
    grads = split(grad_depth)
    grad_mixture = stencil(neighbours(grads), taps[::-1])
    grad_narrow = pool(grad_mixture).astype(BF16)
    next2 = gain2 * old2 + dot_nt(grad_narrow, up_ref[0])
    next1 = gain1 * total1
    cot1[...] = next1
    cot2[...] = next2
    if full:
        core = where[2]
        here = right_ref.at[0]
        put(here, 0, narrow_total.astype(F32))
        put(here, 128, grad_narrow.astype(F32))
        put_two(here, 160, grad_s.astype(F32))
        sums = tap_sums(neighbours(split(mixture_ref[0])), grads)
        put(here, 224, jnp.concatenate(sums + [jnp.zeros((7, C1), F32)], axis=0))
        half = RROWS // 2
        half_ref[0] = right_ref[0, pl.ds(pl.multiple_of(core * half, 8), half), :]
        mixed = join(grad_mixture)

        @pl.when(step == 0)
        def _():
            stem_sum[...] = mixed

        @pl.when(step != 0)
        def _():
            stem_sum[...] = stem_sum[...] + mixed

    @pl.when(step == 3)
    def _():
        put(out_ref, 0, next1)
        put_two(out_ref, 128, next2)
        if full:
            mine = stem_sum[pl.ds(pl.multiple_of(where[2] * 64, 8), 64), :]
            stem_out[:, 0:C1] = mine
            stem_out[:, C1:PAD1] = jnp.zeros((64, PAD1 - C1), F32)


def weight_kernel(where, lo, l1, l2, l3, m1, m2, m3, ro, r1, r2, r3, s1, s2, s3, out_ref, left, right):
    core, block = where[2], where[3]
    for full_ref, own, pairs, rows in (
        (left, lo, ((l1, m2), (l2, m1), (l3, m3)), LROWS),
        (right, ro, ((r1, s2), (r2, s1), (r3, s3)), RROWS),
    ):
        half = rows // 2
        mine = pl.ds(pl.multiple_of(core * half, 8), half)
        other = pl.ds(pl.multiple_of((1 - core) * half, 8), half)
        full_ref[0] = own[0]
        for at, (near, far) in enumerate(pairs):
            full_ref[at + 1, mine, :] = near[0]
            full_ref[at + 1, other, :] = far[0]

    def stack(ref, row, count):
        return jnp.concatenate([ref[q, row : row + count, :] for q in range(4)], axis=0)

    back1 = lax.rem(PAD1 - 45 * block, PAD1)
    back2 = lax.rem(2 * PAD1 - 90 * block, 2 * PAD1)
    hidden = pltpu.roll(stack(left, 0, 128), back1, 1)[:, 0:128].astype(BF16)
    pooled = pltpu.roll(stack(left, 128, 32), back1, 1)[:, 0:128].astype(BF16)
    narrow = jnp.concatenate([stack(left, 160, 32), stack(left, 192, 32)], axis=1)
    narrow = pltpu.roll(narrow, back2, 1)[:, 0:128].astype(BF16)
    grad_mix = dot_tn(hidden, stack(right, 0, 128).astype(BF16))
    grad_up = dot_tn(narrow, stack(right, 128, 32).astype(BF16))
    grad_lo = dot_tn(pooled, stack(right, 160, 32).astype(BF16))
    grad_hi = dot_tn(pooled, stack(right, 192, 32).astype(BF16))
    taps = right[0, 224:240, :] + right[1, 224:240, :] + right[2, 224:240, :] + right[3, 224:240, :]
    out_ref[0, 0:96, :] = grad_up[0:96]
    out_ref[0, 96:144, :] = grad_mix[0:48]
    out_ref[0, 144:192, :] = grad_lo[0:48]
    out_ref[0, 192:240, :] = grad_hi[0:48]
    out_ref[0, 240:256, :] = pltpu.roll(taps, back1, 1)


def final_kernel(own, near, far, up_ref, mix_ref, down_ref, tap_ref):
    total = own[0] + near[...] + far[...]
    up_ref[0] = total[0:90, 0:C1]
    mix_ref[0] = total[96:141, 0:C1]
    down_ref[0, :, 0:PAD1] = total[144:189]
    down_ref[0, :, PAD1:C2] = total[192:237, 0 : C2 - PAD1]
    tap_ref[0] = total[240:249, 0:45]


def shape(*dims, kind=F32):
    return jax.ShapeDtypeStruct(dims, kind)


SMEM = pl.BlockSpec(memory_space=pltpu.SMEM)
WHOLE = pl.BlockSpec(memory_space=pltpu.VMEM)


def shards(stem, labels, up_proj, mix_proj, down_proj, dw_kernel, gain1, gain2, lat_one, lat_two, classifier):
    y, z = lax.axis_index("y"), lax.axis_index("z")
    core = lax.axis_index("core")
    block = lax.axis_index("xl") * 4 + core * 2 + lax.axis_index("xh")
    where = jnp.stack([y, z, core, block]).astype(jnp.int32)
    sign = 1 - 2 * core

    def z_ring(step):
        return [
            (2 * at + c, 2 * ((at + (step if c == 0 else -step)) % 4) + c) for at in range(4) for c in range(2)
        ]

    def x_spot(x, c):
        return ((x % 2) * 2 + c) * 2 + x // 2

    def x_ring(step):
        return [
            (x_spot(x, c), x_spot((x + (step if c == 0 else -step)) % 4, c)) for x in range(4) for c in range(2)
        ]

    z_axes, x_axes = ("z", "core"), ("xl", "core", "xh")

    def swap(values):
        return lax.ppermute(values, "core", [(0, 1), (1, 0)])

    def gather(half, axes, ring):
        near = lax.ppermute(half, axes, ring(1))
        away = lax.ppermute(half, axes, ring(-1))
        opposite = lax.ppermute(near, axes, ring(1))
        return near, away, opposite, swap(near), swap(away), swap(opposite)

    piece = lax.dynamic_index_in_dim(stem, z, 0, keepdims=False).astype(F32)
    marks = lax.dynamic_index_in_dim(labels, z, 0, keepdims=False).astype(F32)
    piece = jnp.concatenate([piece, marks[..., None], jnp.zeros((2, 32, PAD1 - C1 - 1), F32)], axis=-1)
    piece = piece.reshape(2, 16, 2, PAD1).transpose(0, 2, 1, 3).reshape(64, PAD1)
    pairs = [(c, s) for c in range(2) for s in range(2)]
    same = lax.ppermute(piece, ("core", "xh"), [(2 * c + s, 2 * s + c) for c, s in pairs])
    cross = lax.ppermute(piece, ("core", "xh"), [(2 * c + s, 2 * (1 - s) + c) for c, s in pairs])
    crop = jnp.where(core == 0, jnp.concatenate([same, cross], 0), jnp.concatenate([cross, same], 0))

    half = pl.pallas_call(
        pack_kernel,
        out_shape=shape(WROWS, 2 * PAD1),
        in_specs=[SMEM] + [WHOLE] * 6,
        out_specs=WHOLE,
        compiler_params=params(),
        name="pack",
    )(where, up_proj, mix_proj, down_proj, dw_kernel, gain1, gain2)
    pieces = gather(half, z_axes, z_ring)
    weights = pl.pallas_call(
        unpack_kernel,
        out_shape=(
            shape(4, C2, C1, kind=BF16),
            shape(4, C1, C1, kind=BF16),
            shape(4, C1, C2, kind=BF16),
            shape(4, 8, 2 * PAD1),
        ),
        in_specs=[SMEM] + [WHOLE] * 8,
        out_specs=(WHOLE,) * 4,
        compiler_params=params(),
        name="unpack",
    )(where, half, swap(half), *pieces)

    def per(*dims, flip=False):
        zeros = (0,) * len(dims)
        if flip:
            return pl.BlockSpec((1,) + dims, lambda j: (3 - j,) + zeros)
        return pl.BlockSpec((1,) + dims, lambda j: (j,) + zeros)

    def fixed(*dims):
        return pl.BlockSpec(dims, lambda j: (0,) * len(dims))

    def weight_specs(flip):
        return [per(C2, C1, flip=flip), per(C1, C1, flip=flip), per(C1, C2, flip=flip), per(8, 2 * PAD1, flip=flip)]

    def forward(msg, full):
        outs, specs = [shape(192, PAD1)], [fixed(192, PAD1)]
        if full:
            for dims in ((128, C1), (128, C1), (32, C2), (LROWS, PAD1), (LROWS // 2, PAD1)):
                outs.append(shape(4, *dims))
                specs.append(per(*dims))
        return pl.pallas_call(
            lambda *refs: forward_kernel(full, *refs),
            grid=(4,),
            out_shape=tuple(outs),
            in_specs=[SMEM, fixed(192, PAD1), fixed(128, PAD1)] + weight_specs(False),
            out_specs=tuple(specs),
            scratch_shapes=[pltpu.VMEM((128, C1), F32), pltpu.VMEM((32, C2), F32)],
            compiler_params=params(),
            name="forward_full" if full else "forward_light",
        )(where, msg, crop, *weights)

    msg = jnp.zeros((192, PAD1), F32)
    for tick in range(3):
        msg = lax.ppermute(forward(msg, False)[0], "y", [(0, 1), (1, 2), (2, 3)])
    msg, mixture, slope1, slope2, left, left_half = forward(msg, True)
    lefts = gather(left_half, x_axes, x_ring)

    head = pl.pallas_call(
        head_kernel,
        out_shape=shape(192, PAD1),
        in_specs=[SMEM] + [WHOLE] * 5,
        out_specs=WHOLE,
        scratch_shapes=[pltpu.VMEM((128, HEAD), F32), pltpu.VMEM((32, HEAD), F32)],
        compiler_params=params(),
        name="head",
    )(where, msg, crop, lat_one, lat_two, jnp.pad(classifier, ((0, 0), (0, 256 - CLASSES))))

    def backward(msg, full):
        outs, specs = [shape(192, PAD1)], [fixed(192, PAD1)]
        operands = [where, msg, head, slope1, slope2, *weights]
        in_specs = [SMEM, fixed(192, PAD1), fixed(192, PAD1), per(128, C1, flip=True), per(32, C2, flip=True)]
        in_specs += weight_specs(True)
        scratch = [pltpu.VMEM((128, C1), F32), pltpu.VMEM((32, C2), F32)]
        if full:
            operands.append(mixture)
            in_specs.append(per(128, C1, flip=True))
            for dims in ((RROWS, PAD1), (RROWS // 2, PAD1)):
                outs.append(shape(4, *dims))
                specs.append(per(*dims, flip=True))
            outs.append(shape(64, PAD1))
            specs.append(fixed(64, PAD1))
            scratch.append(pltpu.VMEM((128, C1), F32))
        return pl.pallas_call(
            lambda *refs: backward_kernel(full, *refs),
            grid=(4,),
            out_shape=tuple(outs),
            in_specs=in_specs,
            out_specs=tuple(specs),
            scratch_shapes=scratch,
            compiler_params=params(),
            name="backward_full" if full else "backward_light",
        )(*operands)

    cots = head
    for tick in range(3):
        cots = lax.ppermute(backward(cots, False)[0], "y", [(1, 0), (2, 1), (3, 2)])
    _, right, right_half, stem_part = backward(cots, True)
    rights = gather(right_half, x_axes, x_ring)

    order = jnp.stack([z + sign + 4, z - sign + 4, z + 2, z]) % 4
    spots = jnp.concatenate([where, order.astype(jnp.int32)])

    def pick(*dims):
        return pl.BlockSpec((1,) + dims, lambda j, at: (at[4 + j], 0, 0))

    partial = pl.pallas_call(
        weight_kernel,
        grid_spec=pltpu.PrefetchScalarGridSpec(
            num_scalar_prefetch=1,
            grid=(4,),
            in_specs=[pick(LROWS, PAD1)]
            + [pick(LROWS // 2, PAD1)] * 6
            + [pick(RROWS, PAD1)]
            + [pick(RROWS // 2, PAD1)] * 6,
            out_specs=pl.BlockSpec((1, GROWS, PAD1), lambda j, at: (j, 0, 0)),
            scratch_shapes=[pltpu.VMEM((4, LROWS, PAD1), F32), pltpu.VMEM((4, RROWS, PAD1), F32)],
        ),
        out_shape=shape(4, GROWS, PAD1),
        compiler_params=params(),
        name="weight_grads",
    )(spots, left, *lefts, right, *rights)
    relay = lax.ppermute(partial[2], z_axes, z_ring(1))
    away = lax.ppermute(partial[1], z_axes, z_ring(-1))
    near = lax.ppermute(partial[0] + relay, z_axes, z_ring(1))
    grads = pl.pallas_call(
        final_kernel,
        out_shape=(shape(1, 90, C1), shape(1, 45, C1), shape(1, 45, C2), shape(1, 9, 45)),
        in_specs=[WHOLE] * 3,
        out_specs=(WHOLE,) * 4,
        compiler_params=params(),
        name="final",
    )(partial[3:4], near, away)

    cells = stem_part.reshape(4, 16, PAD1).transpose(1, 0, 2)
    cells = lax.all_to_all(cells, ("y", "z"), 0, 0, tiled=True)
    cells = cells.reshape(4, 4, 4, PAD1).sum(axis=0)
    cells = lax.ppermute(cells, ("core", "xh"), [(2 * k + h, 2 * h + k) for k, h in pairs])
    grad_stem = cells[..., 0:C1].reshape(4, 2, 2, C1)
    return (*grads, grad_stem)


def solution(mesh):
    fine = Mesh(mesh.devices.reshape(4, 4, 2, 2, 2), ("y", "z", "xl", "core", "xh"))
    col, dp, strip, both = ("y", "z"), ("xl", "core"), "xh", ("xl", "core", "xh")
    return jax.shard_map(
        shards,
        mesh=fine,
        in_specs=(
            P(dp, strip, None, None),
            P(dp, strip, None),
            P(col, None, None),
            P(col, None, None),
            P(col, None, None),
            P(col, None, None),
            P(col, None),
            P(col, None),
            P(),
            P(),
            P(),
        ),
        out_specs=(
            P(col, both, None),
            P(col, both, None),
            P(col, both, None),
            P(col, None, both),
            P(dp, strip, col, None),
        ),
        check_vma=False,
    )
```

```python
import jax
import jax.numpy as jnp
from jax import lax
from jax.experimental import pallas as pl
from jax.experimental.pallas import tpu as pltpu
from jax.sharding import Mesh, PartitionSpec as P

loss_scale = 64.0
root_coef = 0.7978845608028654
cube_coef = 0.044715

C1 = 360
C2 = 720
PAD1 = 384
HEAD = 512
CLASSES = 150
F32 = jnp.float32
BF16 = jnp.bfloat16
VMEM_LIMIT = 16 * 2**20

WROWS = 464
QROWS = 64
AROWS = WROWS - 4 * QROWS
LROWS = 224
RROWS = 240
GROWS = 256


def params():
    return pltpu.CompilerParams(vmem_limit_bytes=VMEM_LIMIT)


def gelu_pair(values):
    inner = root_coef * (values + cube_coef * values * values * values)
    tangent = jnp.tanh(inner)
    result = 0.5 * values * (1.0 + tangent)
    slope = 0.5 * (1.0 + tangent) + 0.5 * values * (1.0 - tangent * tangent) * root_coef * (
        1.0 + 3.0 * cube_coef * values * values
    )
    return result, slope


def gelu_only(values):
    inner = root_coef * (values + cube_coef * values * values * values)
    return 0.5 * values * (1.0 + jnp.tanh(inner))


def dot(left, right):
    return jnp.dot(left, right, preferred_element_type=F32)


def dot_nt(left, right):
    return lax.dot_general(left, right, (((1,), (1,)), ((), ())), preferred_element_type=F32)


def dot_tn(left, right):
    return lax.dot_general(left, right, (((0,), (0,)), ((), ())), preferred_element_type=F32)


def shifted(even, odd):
    spot = lax.broadcasted_iota(jnp.int32, even.shape, 0)
    after = jnp.where(spot == 15, 0.0, pltpu.roll(even, 15, 0))
    before = jnp.where(spot == 0, 0.0, pltpu.roll(odd, 1, 0))
    return after, before


def neighbours(blocks):
    rows = []
    for r in range(4):
        even, odd = blocks[2 * r], blocks[2 * r + 1]
        after, before = shifted(even, odd)
        rows.append(((before, even, odd), (even, odd, after)))
    return rows


def stencil(rows, taps):
    out = []
    for r in range(4):
        for b in range(2):
            total = None
            for i in (-1, 0, 1):
                if 0 <= r + i < 4:
                    for j in range(3):
                        term = taps[3 * (i + 1) + j] * rows[r + i][b][j]
                        total = term if total is None else total + term
            out.append(total)
    return out


def tap_sums(rows, grads):
    sums = []
    for i in (-1, 0, 1):
        for j in range(3):
            total = None
            for r in range(4):
                if 0 <= r + i < 4:
                    for b in range(2):
                        term = rows[r + i][b][j] * grads[2 * r + b]
                        total = term if total is None else total + term
            sums.append(jnp.sum(total, axis=0, keepdims=True))
    return sums


def pool(blocks):
    parts = [blocks[4 * q] + blocks[4 * q + 1] + blocks[4 * q + 2] + blocks[4 * q + 3] for q in range(2)]
    return jnp.concatenate(parts, axis=0)


def split(values):
    return [values[16 * q : 16 * q + 16] for q in range(8)]


def join(blocks):
    return jnp.concatenate(blocks, axis=0)


def up2(values):
    return [values[16 * (q // 4) : 16 * (q // 4) + 16] for q in range(8)]


def decode_aux(aux):
    taps = [aux[t : t + 1, 0:C1] for t in range(8)] + [aux[0:1, PAD1 : PAD1 + C1]]
    gain1 = aux[1:2, PAD1 : PAD1 + C1]
    gain2 = jnp.concatenate([aux[2:3, PAD1 : 2 * PAD1], aux[3:4, PAD1:C2]], axis=1)
    return taps, gain1, gain2


def put(ref, row, values):
    width = values.shape[1]
    if width < PAD1:
        values = jnp.concatenate([values, jnp.zeros((values.shape[0], PAD1 - width), F32)], axis=1)
    ref[row : row + values.shape[0], :] = values


def put_two(ref, row, values):
    put(ref, row, values[:, 0:PAD1])
    put(ref, row + values.shape[0], values[:, PAD1:C2])


def get_two(ref, row):
    return jnp.concatenate([ref[row : row + 32, :], ref[row + 32 : row + 64, 0 : C2 - PAD1]], axis=1)


def pack_kernel(where, up_hbm, mix_hbm, down_hbm, tap_hbm, g1_hbm, g2_hbm, out_ref, straight_ref, quarter_ref, up_ref, mix_ref, down_ref, tap_ref, g1_ref, g2_ref, sems):
    core = where[2]
    pairs = (
        (up_hbm, up_ref), (mix_hbm, mix_ref), (down_hbm, down_ref), (tap_hbm, tap_ref), (g1_hbm, g1_ref), (g2_hbm, g2_ref)
    )
    copies = [pltpu.make_async_copy(src, dst, sems.at[at]) for at, (src, dst) in enumerate(pairs)]
    for copy in copies:
        copy.start()
    for copy in copies:
        copy.wait()
    mix = mix_ref[0].astype(F32)

    @pl.when(core == 0)
    def _():
        up = up_ref[0].astype(F32)
        out_ref[0:368, 0:C1] = up[0:368]
        out_ref[0:352, PAD1 : PAD1 + C1] = up[368:720]
        out_ref[368:464, 0:C1] = mix[0:96]
        out_ref[368:464, PAD1 : PAD1 + C1] = mix[96:192]

    @pl.when(core == 1)
    def _():
        down = down_ref[0].astype(F32)
        taps = tap_ref[0].astype(F32)
        out_ref[0:360, 0:C2] = down
        out_ref[360:368, 0:C1] = taps[0:8]
        out_ref[360:361, PAD1 : PAD1 + C1] = taps[8:9]
        out_ref[361:362, PAD1 : PAD1 + C1] = g1_ref[...]
        out_ref[362:363, PAD1 : 2 * PAD1] = g2_ref[:, 0:PAD1]
        out_ref[363:364, PAD1:C2] = g2_ref[:, PAD1:C2]
        out_ref[368:464, 0:C1] = mix[192:288]
        out_ref[368:440, PAD1 : PAD1 + C1] = mix[288:360]

    straight_ref[...] = out_ref[0:AROWS, :]
    quarter_ref[...] = out_ref[pl.ds(pl.multiple_of(AROWS + where[3] * QROWS, 8), QROWS), :]


def write_column(first, second, at, up_ref, mix_ref, down_ref, aux_ref):
    up = jnp.concatenate([first[0:368, 0:C1], first[0:352, PAD1 : PAD1 + C1]], axis=0)
    up_ref[at] = up.astype(BF16)
    mix = jnp.concatenate(
        [
            first[368:464, 0:C1],
            first[368:464, PAD1 : PAD1 + C1],
            second[368:464, 0:C1],
            second[368:440, PAD1 : PAD1 + C1],
        ],
        axis=0,
    )
    mix_ref[at] = mix.astype(BF16)
    down_ref[at] = second[0:360, 0:C2].astype(BF16)
    aux_ref[at] = second[360:368, :]


def join_kernel(first, second, third, out_ref):
    for at, ref in enumerate((first, second, third)):
        out_ref[QROWS * at : QROWS * at + QROWS, :] = ref[...]


def add_kernel(first, second, out_ref):
    out_ref[...] = first[...] + second[...]


def own_kernel(where, half, mate, *refs):
    outs, parts, sems = refs[0:4], refs[4:8], refs[8]

    @pl.when(where[2] == 0)
    def _():
        write_column(half, mate, 0, *parts)

    @pl.when(where[2] == 1)
    def _():
        write_column(mate, half, 0, *parts)

    copies = [pltpu.make_async_copy(parts[k].at[0], outs[k].at[where[1]], sems.at[k]) for k in range(4)]
    for copy in copies:
        copy.start()
    for copy in copies:
        copy.wait()


def others_kernel(where, *refs):
    mine, theirs, refs = refs[0:7], refs[7:14], refs[18:]
    outs, parts, halves, sems = refs[0:4], refs[4:8], refs[8], refs[9]
    core, spot = where[2], where[3]
    sign = 1 - 2 * core

    for at in range(3):
        for pieces, hand, place, which in ((mine, sign, core, at), (theirs, -sign, 1 - core, (1, 0, 2)[at])):
            halves[place, 0:AROWS, :] = pieces[which][...]
            for quarters, shift in zip(pieces[3:7], (0, 1, -1, 2)):
                source = lax.rem(spot + 4 - hand * shift, 4)
                rows = pl.ds(pl.multiple_of(AROWS + source * QROWS, 8), QROWS)
                halves[place, rows, :] = quarters[QROWS * which : QROWS * which + QROWS, :]
        write_column(halves.at[0], halves.at[1], at, *parts)
        column = lax.rem(where[1] + 4 - sign * (1, -1, 2)[at], 4)
        for k in range(4):
            pltpu.make_async_copy(parts[k].at[at], outs[k].at[column], sems.at[at, k]).start()
    for at in range(3):
        column = lax.rem(where[1] + 4 - sign * (1, -1, 2)[at], 4)
        for k in range(4):
            pltpu.make_async_copy(parts[k].at[at], outs[k].at[column], sems.at[at, k]).wait()


def hand_over(where, column, factors, slots):
    half = factors.shape[0] // 2
    for at in range(3):

        @pl.when(column == where[4 + at])
        def _(at=at):
            slots[at][0:half, :] = factors[pl.ds(pl.multiple_of(where[2] * half, 8), half), :]

    @pl.when(column == where[1])
    def _():
        slots[3][...] = factors[...]


def take(where, halves, whole):
    core = where[2]
    whole[pl.ds(pl.multiple_of(core * 96, 8), 96), :] = halves[0][...]
    whole[pl.ds(pl.multiple_of((1 - core) * 96, 8), 96), :] = halves[1][...]
    return whole[0:128, 0:C1], get_two(whole, 128)


def give(where, first, second, whole, half):
    put(whole, 0, first)
    put_two(whole, 128, second)
    half[...] = whole[pl.ds(pl.multiple_of(where[2] * 96, 8), 96), :]


def read_crop(where, same, cross, crop):
    crop[pl.ds(pl.multiple_of(where[2] * 64, 8), 64), :] = same[...]
    crop[pl.ds(pl.multiple_of((1 - where[2]) * 64, 8), 64), :] = cross[...]


def forward_kernel(opening, full, where, *refs):
    if opening:
        state1, state2 = jnp.zeros((128, C1), F32), jnp.zeros((32, C2), F32)
    else:
        state1, state2 = take(where, refs[0:2], refs[-1])
        refs = refs[2:]
    same_ref, cross_ref, up_ref, mix_ref, down_ref, aux_ref, out_ref, *rest = refs
    crop_ref, whole = refs[-2:]
    read_crop(where, same_ref, cross_ref, crop_ref)
    if full:
        mixture_ref, slope1_ref, slope2_ref, *slots = rest[:-3]
        factors = rest[-3]
    for column in range(4):
        taps, gain1, gain2 = decode_aux(aux_ref[column])
        narrow = state2.astype(BF16)
        ups = up2(dot(narrow, up_ref[column]))
        mixture = [crop_ref[16 * q : 16 * q + 16, 0:C1] + ups[q] for q in range(8)]
        depth = join(stencil(neighbours(mixture), taps))
        if full:
            active, slope1 = gelu_pair(depth)
        else:
            active = gelu_only(depth)
        hidden = active.astype(BF16)
        state1 = gain1 * state1 + dot(hidden, mix_ref[column])
        pooled = (pool(split(state1)) * 0.25).astype(BF16)
        lifted = dot(pooled, down_ref[column])
        if full:
            active2, slope2 = gelu_pair(lifted)
        else:
            active2 = gelu_only(lifted)
        state2 = gain2 * state2 + active2
        if full:
            mixture_ref[column] = join(mixture)
            slope1_ref[column] = slope1
            slope2_ref[column] = slope2
            put(factors, 0, hidden.astype(F32))
            put(factors, 128, pooled.astype(F32))
            put_two(factors, 160, narrow.astype(F32))
            hand_over(where, column, factors, slots)
    if full:
        put(out_ref, 0, state1)
        put_two(out_ref, 128, state2)
    else:
        give(where, state1, state2, whole, out_ref)


def head_kernel(where, msg_ref, same_ref, cross_ref, one_ref, two_ref, cls_ref, out_ref, first, second, crop_ref):
    read_crop(where, same_ref, cross_ref, crop_ref)
    state1 = msg_ref[0:128, 0:C1].astype(BF16)
    state2 = get_two(msg_ref, 128).astype(BF16)
    labels = crop_ref[:, C1 : C1 + 1].astype(jnp.int32)
    second[...] = dot(state2, two_ref[...])
    first[...] = dot(state1, one_ref[...])
    lateral = first[...] + join(up2(second[...]))
    active, slope = gelu_pair(lateral)
    logits = dot_nt(active.astype(BF16), cls_ref[...])
    classes = lax.broadcasted_iota(jnp.int32, logits.shape, 1)
    logits = logits - jnp.max(logits, axis=-1, keepdims=True)
    powers = jnp.exp(logits)
    probs = powers / jnp.sum(powers, axis=-1, keepdims=True)
    onehot = (classes == labels).astype(F32)
    grad_logits = (probs - onehot) * (loss_scale / 2048.0)
    grad_lat = dot(grad_logits.astype(BF16), cls_ref[...]) * slope
    put(out_ref, 0, dot_nt(grad_lat.astype(BF16), one_ref[...]))
    put_two(out_ref, 128, dot_nt(pool(split(grad_lat)).astype(BF16), two_ref[...]))


def backward_kernel(opening, full, where, *refs):
    if opening:
        head_ref, *refs = refs
        cot1, cot2 = head_ref[0:128, 0:C1], get_two(head_ref, 128)
    else:
        near, far, head_ref, *refs = refs
        cot1, cot2 = take(where, (near, far), refs[-1])
        last = where[0] == 3
        cot1 = jnp.where(last, head_ref[0:128, 0:C1], cot1)
        cot2 = jnp.where(last, get_two(head_ref, 128), cot2)
    slope1_ref, slope2_ref, up_ref, mix_ref, down_ref, aux_ref, *rest = refs
    if full:
        mixture_ref, *slots, stem_own, factors, stem_sum, whole = rest
    else:
        out_ref, whole = rest
    for column in (3, 2, 1, 0):
        taps, gain1, gain2 = decode_aux(aux_ref[column])
        grad_s = (cot2 * slope2_ref[column]).astype(BF16)
        back = dot_nt(grad_s, down_ref[column]) * 0.25
        total1 = cot1 + join(up2(back))
        narrow_total = total1.astype(BF16)
        grad_depth = dot_nt(narrow_total, mix_ref[column]) * slope1_ref[column]
        grads = split(grad_depth)
        grad_mixture = stencil(neighbours(grads), taps[::-1])
        grad_narrow = pool(grad_mixture).astype(BF16)
        if not full or column > 0:
            cot2 = gain2 * cot2 + dot_nt(grad_narrow, up_ref[column])
            cot1 = gain1 * total1
        if full:
            put(factors, 0, narrow_total.astype(F32))
            put(factors, 128, grad_narrow.astype(F32))
            put_two(factors, 160, grad_s.astype(F32))
            sums = tap_sums(neighbours(split(mixture_ref[column])), grads)
            put(factors, 224, jnp.concatenate(sums + [jnp.zeros((7, C1), F32)], axis=0))
            hand_over(where, column, factors, slots)
            mixed = join(grad_mixture)
            stem_sum[...] = mixed if column == 3 else stem_sum[...] + mixed
    if full:
        mine = stem_sum[pl.ds(pl.multiple_of(where[2] * 64, 8), 64), :]
        mine = jnp.concatenate([mine, jnp.zeros((64, PAD1 - C1), F32)], axis=1)
        targets = [(where[4 + at], slots[at].at[RROWS // 2 :]) for at in range(3)] + [(where[1], stem_own)]
        for cell in range(4):
            rows = [16 * q + 4 * y + cell for y in range(4) for q in range(4)]
            part = join([mine[row : row + 1] for row in rows])
            for target, ref in targets:

                @pl.when(target == cell)
                def _(part=part, ref=ref):
                    ref[...] = part
    else:
        give(where, cot1, cot2, whole, out_ref)


def weight_kernel(where, lo, l1, l2, l3, m1, m2, m3, ro, r1, r2, r3, s1, s2, s3, stem_own, *rest):
    *outs, c0, c1, c2, c3, left, right = rest
    core = where[2]
    for full_ref, own, pairs, rows in (
        (left, lo, ((l1, m2), (l2, m1), (l3, m3)), LROWS),
        (right, ro, ((r1, s2), (r2, s1), (r3, s3)), RROWS),
    ):
        half = rows // 2
        mine = pl.ds(pl.multiple_of(core * half, 8), half)
        other = pl.ds(pl.multiple_of((1 - core) * half, 8), half)
        full_ref[0] = own[...]
        for at, (near, far) in enumerate(pairs):
            full_ref[at + 1, mine, :] = near[0:half, :]
            full_ref[at + 1, other, :] = far[0:half, :]

    def stack(ref, row, count):
        return jnp.concatenate([ref[q, row : row + count, :] for q in range(4)], axis=0)

    hidden = stack(left, 0, 128)
    pooled = stack(left, 128, 32)
    narrow = jnp.concatenate([stack(left, 160, 32), stack(left, 192, 32)], axis=1)
    total = stack(right, 0, 128).astype(BF16)
    grad_narrow = stack(right, 128, 32).astype(BF16)
    grad_lo = stack(right, 160, 32).astype(BF16)
    grad_hi = stack(right, 192, 32).astype(BF16)
    taps = right[0, 224:240, :] + right[1, 224:240, :] + right[2, 224:240, :] + right[3, 224:240, :]
    for at, out_ref in enumerate(outs):
        block = where[7 + at]
        back1 = lax.rem(PAD1 - 45 * block, PAD1)
        back2 = lax.rem(2 * PAD1 - 90 * block, 2 * PAD1)
        some_hidden = pltpu.roll(hidden, back1, 1)[:, 0:128].astype(BF16)
        some_pooled = pltpu.roll(pooled, back1, 1)[:, 0:128].astype(BF16)
        some_narrow = pltpu.roll(narrow, back2, 1)[:, 0:128].astype(BF16)
        out_ref[0:96, :] = dot_tn(some_narrow, grad_narrow)[0:96]
        out_ref[96:144, :] = dot_tn(some_hidden, total)[0:48]
        out_ref[144:192, :] = dot_tn(some_pooled, grad_lo)[0:48]
        out_ref[192:240, :] = dot_tn(some_pooled, grad_hi)[0:48]
        out_ref[240:256, :] = pltpu.roll(taps, back1, 1)
    z, sign, skip = where[1], 1 - 2 * core, RROWS // 2
    sources = ((stem_own, 0, z), (r1, skip, z - sign), (r2, skip, z + sign), (r3, skip, z + 2))
    for ref, row, source in sources:
        for cell in range(4):
            part = ref[row + 4 * cell : row + 4 * cell + 4, :]
            for shift, out_ref in enumerate((c0, c1, c2, c3)):

                @pl.when(lax.rem(where[0] + shift, 4) == cell)
                def _(part=part, out_ref=out_ref, source=source):
                    out_ref[lax.rem(source + 4, 4)] = part


def final_kernel(where, own, near, far, c0, c1, c2, c3, up_ref, mix_ref, down_ref, tap_ref, stem_ref):
    total = own[...] + near[...] + far[...]
    up_ref[:, 0, :] = total[0:90, 0:C1]
    mix_ref[:, 0, :] = total[96:141, 0:C1]
    down_ref[:, 0, 0:PAD1] = total[144:189]
    down_ref[:, 0, PAD1:C2] = total[192:237, 0 : C2 - PAD1]
    tap_ref[:, 0, :] = total[240:249, 0:45]
    cells = c0[...] + c1[...] + c2[...] + c3[...]
    stem_ref[:, 0] = cells[:, 0:2, 0:C1]
    stem_ref[:, 1] = cells[:, 2:4, 0:C1]


def shape(*dims, kind=F32):
    return jax.ShapeDtypeStruct(dims, kind)


SMEM = pl.BlockSpec(memory_space=pltpu.SMEM)
WHOLE = pl.BlockSpec(memory_space=pltpu.VMEM)
ANY = pl.BlockSpec(memory_space=pl.ANY)
HBM = pl.BlockSpec(memory_space=pltpu.HBM)


def shards(stem, labels, up_proj, mix_proj, down_proj, dw_kernel, gain1, gain2, lat_one, lat_two, classifier):
    y, z = lax.axis_index("y"), lax.axis_index("z")
    core = lax.axis_index("core")
    sign = 1 - 2 * core
    spot = lax.axis_index("xh") * 2 + lax.axis_index("xl")

    def around(at):
        return [(at + sign + 4) % 4, (at - sign + 4) % 4, (at + 2) % 4]

    blocks = [(x % 2) * 4 + core * 2 + x // 2 for x in around(spot) + [spot]]
    where = jnp.stack([y, z, core, spot, *around(z), *blocks]).astype(jnp.int32)

    def z_ring(step):
        return [
            (2 * at + c, 2 * ((at + (step if c == 0 else -step)) % 4) + c) for at in range(4) for c in range(2)
        ]

    def x_spot(x, c):
        return ((x % 2) * 2 + c) * 2 + x // 2

    def x_ring(step):
        return [
            (x_spot(x, c), x_spot((x + (step if c == 0 else -step)) % 4, c)) for x in range(4) for c in range(2)
        ]

    z_axes, x_axes = ("z", "core"), ("xl", "core", "xh")

    def swap(values):
        return lax.ppermute(values, "core", [(0, 1), (1, 0)])

    def deliver(slots):
        near = lax.ppermute(slots[0], z_axes, z_ring(1))
        away = lax.ppermute(slots[1], z_axes, z_ring(-1))
        opposite = lax.ppermute(slots[2], z_axes, z_ring(2))
        return near, away, opposite

    piece = lax.dynamic_index_in_dim(stem, z, 0, keepdims=False).astype(F32)
    marks = lax.dynamic_index_in_dim(labels, z, 0, keepdims=False).astype(F32)
    piece = jnp.concatenate([piece, marks[..., None], jnp.zeros((2, 32, PAD1 - C1 - 1), F32)], axis=-1)
    piece = piece.reshape(2, 16, 2, PAD1).transpose(0, 2, 1, 3).reshape(64, PAD1)
    where, piece = lax.optimization_barrier((where, piece))
    pairs = [(c, s) for c in range(2) for s in range(2)]
    same = lax.ppermute(piece, ("core", "xh"), [(2 * c + s, 2 * s + c) for c, s in pairs])
    cross = lax.ppermute(piece, ("core", "xh"), [(2 * c + s, 2 * (1 - s) + c) for c, s in pairs])
    weight_dims = ((C2, C1), (C1, C1), (C1, C2))
    half, straight, quarter = pl.pallas_call(
        pack_kernel,
        out_shape=(shape(WROWS, 2 * PAD1), shape(AROWS, 2 * PAD1), shape(QROWS, 2 * PAD1)),
        in_specs=[SMEM] + [HBM] * 6,
        out_specs=(WHOLE,) * 3,
        scratch_shapes=[pltpu.VMEM((1,) + dims, BF16) for dims in weight_dims]
        + [pltpu.VMEM((1, 9, C1), BF16), pltpu.VMEM((1, C1), F32), pltpu.VMEM((1, C2), F32)]
        + [pltpu.SemaphoreType.DMA((6,))],
        compiler_params=params(),
        name="pack",
    )(where, up_proj, mix_proj, down_proj, dw_kernel, gain1, gain2)

    def both_ways(values, axes, ring):
        return lax.ppermute(values, axes, ring(1)), lax.ppermute(values, axes, ring(-1))

    near, away = both_ways(quarter, z_axes, z_ring)
    opposite = lax.ppermute(near, z_axes, z_ring(1))
    near, away, opposite, straight, same, cross = lax.optimization_barrier((near, away, opposite, straight, same, cross))
    quarters = pl.pallas_call(
        join_kernel,
        out_shape=shape(3 * QROWS, 2 * PAD1),
        in_specs=[WHOLE] * 3,
        out_specs=WHOLE,
        compiler_params=params(),
        name="join_quarters",
    )(near, away, opposite)
    straights = both_ways(straight, z_axes, z_ring)
    spread = both_ways(quarters, x_axes, x_ring)
    mine = [
        *straights,
        lax.ppermute(straights[0], z_axes, z_ring(1)),
        quarters,
        *spread,
        lax.ppermute(spread[0], x_axes, x_ring(1)),
    ]
    columns = tuple(shape(4, *dims, kind=BF16) for dims in weight_dims) + (shape(4, 8, 2 * PAD1),)

    def column_scratch(count):
        return [pltpu.VMEM((count,) + dims, BF16) for dims in weight_dims] + [pltpu.VMEM((count, 8, 2 * PAD1), F32)]

    weights = pl.pallas_call(
        own_kernel,
        out_shape=columns,
        in_specs=[SMEM] + [WHOLE] * 2,
        out_specs=(ANY,) * 4,
        scratch_shapes=column_scratch(1) + [pltpu.SemaphoreType.DMA((4,))],
        compiler_params=params(),
        name="own_column",
    )(where, half, swap(half))
    weights = pl.pallas_call(
        others_kernel,
        out_shape=columns,
        in_specs=[SMEM] + [WHOLE] * 14 + [ANY] * 4,
        out_specs=(ANY,) * 4,
        input_output_aliases={15 + k: k for k in range(4)},
        scratch_shapes=column_scratch(3) + [pltpu.VMEM((2, WROWS, 2 * PAD1), F32), pltpu.SemaphoreType.DMA((3, 4))],
        compiler_params=params(),
        name="other_columns",
    )(where, *mine, *[swap(part) for part in mine], *weights)

    whole = pltpu.VMEM((192, PAD1), F32)

    def forward(halves, full):
        dims = [(192, PAD1) if full else (96, PAD1)]
        if full:
            dims += [(4, 128, C1), (4, 128, C1), (4, 32, C2)] + [(LROWS // 2, PAD1)] * 3 + [(LROWS, PAD1)]
        return pl.pallas_call(
            lambda *refs: forward_kernel(not halves, full, *refs),
            out_shape=tuple(shape(*each) for each in dims),
            in_specs=[SMEM] + [WHOLE] * (len(halves) + 6),
            out_specs=(WHOLE,) * len(dims),
            scratch_shapes=[pltpu.VMEM((LROWS, PAD1), F32)] * full + [pltpu.VMEM((128, PAD1), F32), whole],
            compiler_params=params(),
            name="forward_full" if full else "forward_light",
        )(where, *halves, same, cross, *weights)

    def hop(half, pairs):
        half = lax.ppermute(half, "y", pairs)
        return half, swap(half)

    halves = ()
    for tick in range(3):
        halves = hop(forward(halves, False)[0], [(0, 1), (1, 2), (2, 3)])
    msg, mixture, slope1, slope2, *lefts, left = forward(halves, True)
    lefts = deliver(lefts)

    head = pl.pallas_call(
        head_kernel,
        out_shape=shape(192, PAD1),
        in_specs=[SMEM] + [WHOLE] * 6,
        out_specs=WHOLE,
        scratch_shapes=[pltpu.VMEM((128, HEAD), F32), pltpu.VMEM((32, HEAD), F32), pltpu.VMEM((128, PAD1), F32)],
        compiler_params=params(),
        name="head",
    )(where, msg, same, cross, lat_one, lat_two, classifier.T)

    def backward(halves, full):
        operands = [*halves, head, slope1, slope2, *weights]
        dims = [(96, PAD1)]
        if full:
            operands.append(mixture)
            dims = [(RROWS // 2 + 16, PAD1)] * 3 + [(RROWS, PAD1), (16, PAD1)]
        return pl.pallas_call(
            lambda *refs: backward_kernel(not halves, full, *refs),
            out_shape=tuple(shape(*each) for each in dims),
            in_specs=[SMEM] + [WHOLE] * len(operands),
            out_specs=(WHOLE,) * len(dims),
            scratch_shapes=[pltpu.VMEM((RROWS, PAD1), F32), pltpu.VMEM((128, C1), F32)] * full + [whole],
            compiler_params=params(),
            name="backward_full" if full else "backward_light",
        )(where, *operands)

    halves = ()
    for tick in range(3):
        halves = hop(backward(halves, False)[0], [(1, 0), (2, 1), (3, 2)])
        if tick == 0:
            halves, lefts = lax.optimization_barrier((halves, lefts))
            mates = [swap(part) for part in lefts]
        if tick == 1:
            halves, mates = lax.optimization_barrier((halves, mates))
    slots = backward(halves, True)
    rights = deliver(slots[0:3])

    *partial, c0, c1, c2, c3 = pl.pallas_call(
        weight_kernel,
        out_shape=(shape(GROWS, PAD1),) * 4 + (shape(4, 4, PAD1),) * 4,
        in_specs=[SMEM] + [WHOLE] * 15,
        out_specs=(WHOLE,) * 8,
        scratch_shapes=[pltpu.VMEM((4, LROWS, PAD1), F32), pltpu.VMEM((4, RROWS, PAD1), F32)],
        compiler_params=params(),
        name="weight_grads",
    )(where, left, *lefts, *mates, slots[3], *rights, *[swap(part) for part in rights], slots[4])
    relay = lax.ppermute(partial[2], x_axes, x_ring(1))
    away = lax.ppermute(partial[1], x_axes, x_ring(-1))
    relay, away, cells = lax.optimization_barrier((relay, away, (c0, c1, c2, c3)))
    passed = pl.pallas_call(
        add_kernel,
        out_shape=shape(GROWS, PAD1),
        in_specs=[WHOLE] * 2,
        out_specs=WHOLE,
        compiler_params=params(),
        name="add_relay",
    )(partial[0], relay)
    near = lax.ppermute(passed, x_axes, x_ring(1))

    def stem_pairs(step):
        return [(4 * at + 2 * k + h, 4 * ((at + step) % 4) + 2 * h + k) for at in range(4) for k, h in pairs]

    cells = [lax.ppermute(cells[step], ("y", "core", "xh"), stem_pairs(step)) for step in range(4)]
    *grads, grad_stem = pl.pallas_call(
        final_kernel,
        out_shape=(shape(90, 1, C1), shape(45, 1, C1), shape(45, 1, C2), shape(9, 1, 45), shape(4, 2, 2, C1)),
        in_specs=[SMEM] + [WHOLE] * 7,
        out_specs=(WHOLE,) * 5,
        compiler_params=params(),
        name="final",
    )(where, partial[3], near, away, *cells)
    return (*[grad.transpose(1, 0, 2) for grad in grads], grad_stem)


def solution(mesh):
    fine = Mesh(mesh.devices.reshape(4, 4, 2, 2, 2), ("y", "z", "xl", "core", "xh"))
    col, dp, strip, both = ("y", "z"), ("xl", "core"), "xh", ("xl", "core", "xh")
    return jax.shard_map(
        shards,
        mesh=fine,
        in_specs=(
            P(dp, strip, None, None),
            P(dp, strip, None),
            P(col, None, None),
            P(col, None, None),
            P(col, None, None),
            P(col, None, None),
            P(col, None),
            P(col, None),
            P(),
            P(),
            P(),
        ),
        out_specs=(
            P(col, both, None),
            P(col, both, None),
            P(col, both, None),
            P(col, None, both),
            P(dp, strip, col, None),
        ),
        check_vma=False,
    )
```

```python
import jax
import jax.numpy as jnp
from jax import lax
from jax.experimental import pallas as pl
from jax.experimental.pallas import tpu as pltpu
from jax.sharding import Mesh, PartitionSpec as P

loss_scale = 64.0
root_coef = 0.7978845608028654
cube_coef = 0.044715

C1 = 360
C2 = 720
PAD1 = 384
HEAD = 512
CLASSES = 150
F32 = jnp.float32
BF16 = jnp.bfloat16
VMEM_LIMIT = 16 * 2**20
PACK_LIMIT = 60 * 2**20

WROWS = 464
QROWS = 64
AROWS = WROWS - 4 * QROWS
LROWS = 224
RROWS = 240
GROWS = 256


def params(limit=VMEM_LIMIT):
    return pltpu.CompilerParams(vmem_limit_bytes=limit)


def gelu_pair(values):
    inner = root_coef * (values + cube_coef * values * values * values)
    tangent = jnp.tanh(inner)
    result = 0.5 * values * (1.0 + tangent)
    slope = 0.5 * (1.0 + tangent) + 0.5 * values * (1.0 - tangent * tangent) * root_coef * (
        1.0 + 3.0 * cube_coef * values * values
    )
    return result, slope


def gelu_only(values):
    inner = root_coef * (values + cube_coef * values * values * values)
    return 0.5 * values * (1.0 + jnp.tanh(inner))


def dot(left, right):
    return jnp.dot(left, right, preferred_element_type=F32)


def dot_nt(left, right):
    return lax.dot_general(left, right, (((1,), (1,)), ((), ())), preferred_element_type=F32)


def dot_tn(left, right):
    return lax.dot_general(left, right, (((0,), (0,)), ((), ())), preferred_element_type=F32)


def shifted(even, odd):
    spot = lax.broadcasted_iota(jnp.int32, even.shape, 0)
    after = jnp.where(spot == 15, 0.0, pltpu.roll(even, 15, 0))
    before = jnp.where(spot == 0, 0.0, pltpu.roll(odd, 1, 0))
    return after, before


def neighbours(blocks):
    rows = []
    for r in range(4):
        even, odd = blocks[2 * r], blocks[2 * r + 1]
        after, before = shifted(even, odd)
        rows.append(((before, even, odd), (even, odd, after)))
    return rows


def stencil(rows, taps):
    out = []
    for r in range(4):
        for b in range(2):
            total = None
            for i in (-1, 0, 1):
                if 0 <= r + i < 4:
                    for j in range(3):
                        term = taps[3 * (i + 1) + j] * rows[r + i][b][j]
                        total = term if total is None else total + term
            out.append(total)
    return out


def tap_sums(rows, grads):
    sums = []
    for i in (-1, 0, 1):
        for j in range(3):
            total = None
            for r in range(4):
                if 0 <= r + i < 4:
                    for b in range(2):
                        term = rows[r + i][b][j] * grads[2 * r + b]
                        total = term if total is None else total + term
            sums.append(jnp.sum(total, axis=0, keepdims=True))
    return sums


def pool(blocks):
    parts = [blocks[4 * q] + blocks[4 * q + 1] + blocks[4 * q + 2] + blocks[4 * q + 3] for q in range(2)]
    return jnp.concatenate(parts, axis=0)


def split(values):
    return [values[16 * q : 16 * q + 16] for q in range(8)]


def join(blocks):
    return jnp.concatenate(blocks, axis=0)


def up2(values):
    return [values[16 * (q // 4) : 16 * (q // 4) + 16] for q in range(8)]


def decode_aux(aux):
    taps = [aux[t : t + 1, 0:C1] for t in range(8)] + [aux[0:1, PAD1 : PAD1 + C1]]
    gain1 = aux[1:2, PAD1 : PAD1 + C1]
    gain2 = jnp.concatenate([aux[2:3, PAD1 : 2 * PAD1], aux[3:4, PAD1:C2]], axis=1)
    return taps, gain1, gain2


def put(ref, row, values):
    width = values.shape[1]
    if width < PAD1:
        values = jnp.concatenate([values, jnp.zeros((values.shape[0], PAD1 - width), F32)], axis=1)
    ref[row : row + values.shape[0], :] = values


def put_two(ref, row, values):
    put(ref, row, values[:, 0:PAD1])
    put(ref, row + values.shape[0], values[:, PAD1:C2])


def get_two(ref, row):
    return jnp.concatenate([ref[row : row + 32, :], ref[row + 32 : row + 64, 0 : C2 - PAD1]], axis=1)


def pack_kernel(where, *refs):
    sources, outs, held, sems = refs[0:8], refs[8:12], refs[12:20], refs[22]
    (half_ref, wide_ref), (straight_ref, quarter_ref, piece_ref, aux_ref) = refs[20:22], outs
    up_ref, mix_ref, down_ref, tap_ref, g1_ref, g2_ref, stem_ref, label_ref = held
    core = where[2]
    copies = [
        pltpu.make_async_copy(src.at[where[1]] if at >= 6 else src, dst, sems.at[at])
        for at, (src, dst) in enumerate(zip(sources, held))
    ]
    for copy in copies:
        copy.start()
    for copy in copies:
        copy.wait()
    mix = mix_ref[0].astype(F32)
    taps = tap_ref[0].astype(F32)
    aux_ref[0:8, 0:C1] = taps[0:8]
    aux_ref[0:1, PAD1 : PAD1 + C1] = taps[8:9]
    aux_ref[1:2, PAD1 : PAD1 + C1] = g1_ref[...]
    aux_ref[2:3, PAD1 : 2 * PAD1] = g2_ref[:, 0:PAD1]
    aux_ref[3:4, PAD1:C2] = g2_ref[:, PAD1:C2]

    @pl.when(core == 0)
    def _():
        up = up_ref[0].astype(F32)
        half_ref[0:368, 0:C1] = up[0:368]
        half_ref[0:352, PAD1 : PAD1 + C1] = up[368:720]
        half_ref[368:464, 0:C1] = mix[0:96]
        half_ref[368:464, PAD1 : PAD1 + C1] = mix[96:192]

    @pl.when(core == 1)
    def _():
        half_ref[0:360, 0:C2] = down_ref[0].astype(F32)
        half_ref[360:368, :] = aux_ref[...]
        half_ref[368:464, 0:C1] = mix[192:288]
        half_ref[368:440, PAD1 : PAD1 + C1] = mix[288:360]

    straight_ref[...] = half_ref[0:AROWS, :]
    quarter_ref[...] = half_ref[pl.ds(pl.multiple_of(AROWS + where[3] * QROWS, 8), QROWS), :]

    wide = jnp.concatenate([stem_ref[...].astype(F32), jnp.zeros((2, 32, PAD1 - C1), F32)], axis=2)
    for part in range(3):
        wide_ref[part] = wide[:, :, 128 * part : 128 * part + 128]
    marks = label_ref[...].astype(F32)
    cell = lax.broadcasted_iota(jnp.int32, (16, 32), 0)
    pixel = lax.broadcasted_iota(jnp.int32, (16, 32), 1)
    lane = lax.broadcasted_iota(jnp.int32, (16, PAD1), 1)
    for a in range(2):
        for b in range(2):
            chosen = jnp.where(pixel == 2 * cell + b, marks[a : a + 1], 0.0)
            mark = jnp.sum(chosen, axis=1, keepdims=True)
            pixels = jnp.concatenate([wide_ref[part, a, pl.ds(b, 16, stride=2), :] for part in range(3)], axis=1)
            piece_ref[32 * a + 16 * b : 32 * a + 16 * b + 16, :] = jnp.where(lane == C1, mark, pixels)


def write_column(first, second, at, up_ref, mix_ref, down_ref, aux_ref):
    up = jnp.concatenate([first[0:368, 0:C1], first[0:352, PAD1 : PAD1 + C1]], axis=0)
    up_ref[at] = up.astype(BF16)
    mix = jnp.concatenate(
        [
            first[368:464, 0:C1],
            first[368:464, PAD1 : PAD1 + C1],
            second[368:464, 0:C1],
            second[368:440, PAD1 : PAD1 + C1],
        ],
        axis=0,
    )
    mix_ref[at] = mix.astype(BF16)
    down_ref[at] = second[0:360, 0:C2].astype(BF16)
    aux_ref[at] = second[360:368, :]


def join_kernel(first, second, third, out_ref):
    for at, ref in enumerate((first, second, third)):
        out_ref[QROWS * at : QROWS * at + QROWS, :] = ref[...]


def add_kernel(first, second, out_ref):
    out_ref[...] = first[...] + second[...]


def columns_kernel(where, *refs):
    mine, theirs, own, refs = refs[0:7], refs[7:14], refs[14:18], refs[18:]
    outs, parts, halves, sems = refs[0:4], refs[4:8], refs[8], refs[9]
    core, spot = where[2], where[3]
    sign = 1 - 2 * core

    def moves(at):
        if at == 3:
            sources = [ref.at[0] for ref in own[0:3]] + [own[3]]
            column = where[1]
        else:
            sources = [ref.at[at] for ref in parts]
            column = lax.rem(where[1] + 4 - sign * (1, -1, 2)[at], 4)
        return [pltpu.make_async_copy(src, outs[k].at[column], sems.at[at, k]) for k, src in enumerate(sources)]

    for move in moves(3):
        move.start()
    for at in range(3):
        for pieces, hand, place, which in ((mine, sign, core, at), (theirs, -sign, 1 - core, (1, 0, 2)[at])):
            halves[place, 0:AROWS, :] = pieces[which][...]
            for quarters, shift in zip(pieces[3:7], (0, 1, -1, 2)):
                source = lax.rem(spot + 4 - hand * shift, 4)
                rows = pl.ds(pl.multiple_of(AROWS + source * QROWS, 8), QROWS)
                halves[place, rows, :] = quarters[QROWS * which : QROWS * which + QROWS, :]
        write_column(halves.at[0], halves.at[1], at, *parts)
        for move in moves(at):
            move.start()
    for at in range(4):
        for move in moves(at):
            move.wait()


def hand_over(where, column, factors, slots):
    half = factors.shape[0] // 2
    for at in range(3):

        @pl.when(column == where[4 + at])
        def _(at=at):
            slots[at][0:half, :] = factors[pl.ds(pl.multiple_of(where[2] * half, 8), half), :]

    @pl.when(column == where[1])
    def _():
        slots[3][...] = factors[...]


def take(where, halves, whole):
    core = where[2]
    whole[pl.ds(pl.multiple_of(core * 96, 8), 96), :] = halves[0][...]
    whole[pl.ds(pl.multiple_of((1 - core) * 96, 8), 96), :] = halves[1][...]


def take_own(where, pairs, planes, start, whole):
    for at, plane in enumerate(planes):

        @pl.when(where[0] == plane)
        def _(at=at):
            take(where, pairs[2 * at : 2 * at + 2], whole)

    @pl.when(where[0] == 6 - sum(planes))
    def _():
        whole[...] = jnp.zeros((192, PAD1), F32) if start is None else start[...]


def unfold(whole):
    return whole[0:128, 0:C1], get_two(whole, 128)


def give(where, first, second, whole, half):
    put(whole, 0, first)
    put_two(whole, 128, second)
    half[...] = whole[pl.ds(pl.multiple_of(where[2] * 96, 8), 96), :]


def read_crop(where, same, cross, crop):
    crop[pl.ds(pl.multiple_of(where[2] * 64, 8), 64), :] = same[...]
    crop[pl.ds(pl.multiple_of((1 - where[2]) * 64, 8), 64), :] = cross[...]


def forward_kernel(opening, full, where, *refs):
    if opening:
        state1, state2 = jnp.zeros((128, C1), F32), jnp.zeros((32, C2), F32)
    elif full:
        take_own(where, refs[0:6], (1, 2, 3), None, refs[-1])
        state1, state2 = unfold(refs[-1])
        refs = refs[6:]
    else:
        take(where, refs[0:2], refs[-1])
        state1, state2 = unfold(refs[-1])
        refs = refs[2:]
    same_ref, cross_ref, up_ref, mix_ref, down_ref, aux_ref, out_ref, *rest = refs
    crop_ref, whole = refs[-2:]
    read_crop(where, same_ref, cross_ref, crop_ref)
    if full:
        mixture_ref, slope1_ref, slope2_ref, *slots = rest[:-3]
        factors = rest[-3]
    for column in range(4):
        taps, gain1, gain2 = decode_aux(aux_ref[column])
        narrow = state2.astype(BF16)
        ups = up2(dot(narrow, up_ref[column]))
        mixture = [crop_ref[16 * q : 16 * q + 16, 0:C1] + ups[q] for q in range(8)]
        depth = join(stencil(neighbours(mixture), taps))
        if full:
            active, slope1 = gelu_pair(depth)
        else:
            active = gelu_only(depth)
        hidden = active.astype(BF16)
        state1 = gain1 * state1 + dot(hidden, mix_ref[column])
        pooled = (pool(split(state1)) * 0.25).astype(BF16)
        lifted = dot(pooled, down_ref[column])
        if full:
            active2, slope2 = gelu_pair(lifted)
        else:
            active2 = gelu_only(lifted)
        state2 = gain2 * state2 + active2
        if full:
            mixture_ref[column] = join(mixture)
            slope1_ref[column] = slope1
            slope2_ref[column] = slope2
            put(factors, 0, hidden.astype(F32))
            put(factors, 128, pooled.astype(F32))
            put_two(factors, 160, narrow.astype(F32))
            hand_over(where, column, factors, slots)
    if full:
        put(out_ref, 0, state1)
        put_two(out_ref, 128, state2)
    else:
        give(where, state1, state2, whole, out_ref)


def head_kernel(where, msg_ref, same_ref, cross_ref, one_ref, two_ref, cls_ref, out_ref, first, second, crop_ref):
    read_crop(where, same_ref, cross_ref, crop_ref)
    state1 = msg_ref[0:128, 0:C1].astype(BF16)
    state2 = get_two(msg_ref, 128).astype(BF16)
    labels = crop_ref[:, C1 : C1 + 1].astype(jnp.int32)
    second[...] = dot(state2, two_ref[...])
    first[...] = dot(state1, one_ref[...])
    lateral = first[...] + join(up2(second[...]))
    active, slope = gelu_pair(lateral)
    logits = dot_nt(active.astype(BF16), cls_ref[...])
    classes = lax.broadcasted_iota(jnp.int32, logits.shape, 1)
    logits = logits - jnp.max(logits, axis=-1, keepdims=True)
    powers = jnp.exp(logits)
    probs = powers / jnp.sum(powers, axis=-1, keepdims=True)
    onehot = (classes == labels).astype(F32)
    grad_logits = (probs - onehot) * (loss_scale / 2048.0)
    grad_lat = dot(grad_logits.astype(BF16), cls_ref[...]) * slope
    put(out_ref, 0, dot_nt(grad_lat.astype(BF16), one_ref[...]))
    put_two(out_ref, 128, dot_nt(pool(split(grad_lat)).astype(BF16), two_ref[...]))


def backward_kernel(opening, full, where, *refs):
    if opening:
        head_ref, *refs = refs
        cot1, cot2 = unfold(head_ref)
    elif full:
        take_own(where, refs[0:6], (2, 1, 0), refs[6], refs[-1])
        cot1, cot2 = unfold(refs[-1])
        refs = refs[7:]
    else:
        take(where, refs[0:2], refs[-1])
        cot1, cot2 = unfold(refs[-1])
        refs = refs[2:]
    slope1_ref, slope2_ref, up_ref, mix_ref, down_ref, aux_ref, *rest = refs
    if full:
        mixture_ref, *slots, stem_own, factors, stem_sum, whole = rest
    else:
        out_ref, whole = rest
    for column in (3, 2, 1, 0):
        taps, gain1, gain2 = decode_aux(aux_ref[column])
        grad_s = (cot2 * slope2_ref[column]).astype(BF16)
        back = dot_nt(grad_s, down_ref[column]) * 0.25
        total1 = cot1 + join(up2(back))
        narrow_total = total1.astype(BF16)
        grad_depth = dot_nt(narrow_total, mix_ref[column]) * slope1_ref[column]
        grads = split(grad_depth)
        grad_mixture = stencil(neighbours(grads), taps[::-1])
        grad_narrow = pool(grad_mixture).astype(BF16)
        if not full or column > 0:
            cot2 = gain2 * cot2 + dot_nt(grad_narrow, up_ref[column])
            cot1 = gain1 * total1
        if full:
            put(factors, 0, narrow_total.astype(F32))
            put(factors, 128, grad_narrow.astype(F32))
            put_two(factors, 160, grad_s.astype(F32))
            sums = tap_sums(neighbours(split(mixture_ref[column])), grads)
            put(factors, 224, jnp.concatenate(sums + [jnp.zeros((7, C1), F32)], axis=0))
            hand_over(where, column, factors, slots)
            mixed = join(grad_mixture)
            stem_sum[...] = mixed if column == 3 else stem_sum[...] + mixed
    if full:
        mine = stem_sum[pl.ds(pl.multiple_of(where[2] * 64, 8), 64), :]
        mine = jnp.concatenate([mine, jnp.zeros((64, PAD1 - C1), F32)], axis=1)
        targets = [(where[4 + at], slots[at].at[RROWS // 2 :]) for at in range(3)] + [(where[1], stem_own)]
        for cell in range(4):
            rows = [16 * q + 4 * y + cell for y in range(4) for q in range(4)]
            part = join([mine[row : row + 1] for row in rows])
            for target, ref in targets:

                @pl.when(target == cell)
                def _(part=part, ref=ref):
                    ref[...] = part
    else:
        give(where, cot1, cot2, whole, out_ref)


def weight_kernel(where, lo, l1, l2, l3, m1, m2, m3, ro, r1, r2, r3, s1, s2, s3, stem_own, *rest):
    *outs, c0, c1, c2, c3, left, right = rest
    core = where[2]
    for full_ref, own, pairs, rows in (
        (left, lo, ((l1, m2), (l2, m1), (l3, m3)), LROWS),
        (right, ro, ((r1, s2), (r2, s1), (r3, s3)), RROWS),
    ):
        half = rows // 2
        mine = pl.ds(pl.multiple_of(core * half, 8), half)
        other = pl.ds(pl.multiple_of((1 - core) * half, 8), half)
        full_ref[0] = own[...]
        for at, (near, far) in enumerate(pairs):
            full_ref[at + 1, mine, :] = near[0:half, :]
            full_ref[at + 1, other, :] = far[0:half, :]

    def stack(ref, row, count):
        return jnp.concatenate([ref[q, row : row + count, :] for q in range(4)], axis=0)

    hidden = stack(left, 0, 128)
    pooled = stack(left, 128, 32)
    narrow = jnp.concatenate([stack(left, 160, 32), stack(left, 192, 32)], axis=1)
    total = stack(right, 0, 128).astype(BF16)
    grad_narrow = stack(right, 128, 32).astype(BF16)
    grad_lo = stack(right, 160, 32).astype(BF16)
    grad_hi = stack(right, 192, 32).astype(BF16)
    taps = right[0, 224:240, :] + right[1, 224:240, :] + right[2, 224:240, :] + right[3, 224:240, :]
    for at, out_ref in enumerate(outs):
        block = where[7 + at]
        back1 = lax.rem(PAD1 - 45 * block, PAD1)
        back2 = lax.rem(2 * PAD1 - 90 * block, 2 * PAD1)
        some_hidden = pltpu.roll(hidden, back1, 1)[:, 0:128].astype(BF16)
        some_pooled = pltpu.roll(pooled, back1, 1)[:, 0:128].astype(BF16)
        some_narrow = pltpu.roll(narrow, back2, 1)[:, 0:128].astype(BF16)
        out_ref[0:96, :] = dot_tn(some_narrow, grad_narrow)[0:96]
        out_ref[96:144, :] = dot_tn(some_hidden, total)[0:48]
        out_ref[144:192, :] = dot_tn(some_pooled, grad_lo)[0:48]
        out_ref[192:240, :] = dot_tn(some_pooled, grad_hi)[0:48]
        out_ref[240:256, :] = pltpu.roll(taps, back1, 1)
    z, sign, skip = where[1], 1 - 2 * core, RROWS // 2
    sources = ((stem_own, 0, z), (r1, skip, z - sign), (r2, skip, z + sign), (r3, skip, z + 2))
    for ref, row, source in sources:
        for cell in range(4):
            part = ref[row + 4 * cell : row + 4 * cell + 4, :]
            for shift, out_ref in enumerate((c0, c1, c2, c3)):

                @pl.when(lax.rem(where[0] + shift, 4) == cell)
                def _(part=part, out_ref=out_ref, source=source):
                    out_ref[lax.rem(source + 4, 4)] = part


def final_kernel(where, own, near, far, c0, c1, c2, c3, up_ref, mix_ref, down_ref, tap_ref, stem_ref):
    total = own[...] + near[...] + far[...]
    up_ref[:, 0, :] = total[0:90, 0:C1]
    mix_ref[:, 0, :] = total[96:141, 0:C1]
    down_ref[:, 0, 0:PAD1] = total[144:189]
    down_ref[:, 0, PAD1:C2] = total[192:237, 0 : C2 - PAD1]
    tap_ref[:, 0, :] = total[240:249, 0:45]
    cells = c0[...] + c1[...] + c2[...] + c3[...]
    stem_ref[:, 0] = cells[:, 0:2, 0:C1]
    stem_ref[:, 1] = cells[:, 2:4, 0:C1]


def shape(*dims, kind=F32):
    return jax.ShapeDtypeStruct(dims, kind)


SMEM = pl.BlockSpec(memory_space=pltpu.SMEM)
WHOLE = pl.BlockSpec(memory_space=pltpu.VMEM)
ANY = pl.BlockSpec(memory_space=pl.ANY)
HBM = pl.BlockSpec(memory_space=pltpu.HBM)


def shards(stem, labels, up_proj, mix_proj, down_proj, dw_kernel, gain1, gain2, lat_one, lat_two, classifier):
    y, z = lax.axis_index("y"), lax.axis_index("z")
    core = lax.axis_index("core")
    sign = 1 - 2 * core
    spot = lax.axis_index("xh") * 2 + lax.axis_index("xl")

    def around(at):
        return [(at + sign + 4) % 4, (at - sign + 4) % 4, (at + 2) % 4]

    blocks = [(x % 2) * 4 + core * 2 + x // 2 for x in around(spot) + [spot]]
    where = jnp.stack([y, z, core, spot, *around(z), *blocks]).astype(jnp.int32)

    def z_ring(step):
        return [
            (2 * at + c, 2 * ((at + (step if c == 0 else -step)) % 4) + c) for at in range(4) for c in range(2)
        ]

    def x_spot(x, c):
        return ((x % 2) * 2 + c) * 2 + x // 2

    def x_ring(step):
        return [
            (x_spot(x, c), x_spot((x + (step if c == 0 else -step)) % 4, c)) for x in range(4) for c in range(2)
        ]

    z_axes, x_axes = ("z", "core"), ("xl", "core", "xh")

    def swap(values):
        return lax.ppermute(values, "core", [(0, 1), (1, 0)])

    def deliver(slots):
        near = lax.ppermute(slots[0], z_axes, z_ring(1))
        away = lax.ppermute(slots[1], z_axes, z_ring(-1))
        opposite = lax.ppermute(slots[2], z_axes, z_ring(2))
        return near, away, opposite

    weight_dims = ((C2, C1), (C1, C1), (C1, C2))
    straight, quarter, piece, aux = pl.pallas_call(
        pack_kernel,
        out_shape=(shape(AROWS, 2 * PAD1), shape(QROWS, 2 * PAD1), shape(64, PAD1), shape(8, 2 * PAD1)),
        in_specs=[SMEM] + [HBM] * 8,
        out_specs=(WHOLE,) * 4,
        scratch_shapes=[pltpu.VMEM((1,) + dims, BF16) for dims in weight_dims]
        + [pltpu.VMEM((1, 9, C1), BF16), pltpu.VMEM((1, C1), F32), pltpu.VMEM((1, C2), F32)]
        + [pltpu.VMEM((2, 32, C1), BF16), pltpu.VMEM((2, 32), jnp.int32)]
        + [pltpu.VMEM((WROWS, 2 * PAD1), F32), pltpu.VMEM((3, 2, 32, 128), F32), pltpu.SemaphoreType.DMA((8,))],
        compiler_params=params(PACK_LIMIT),
        name="pack",
    )(where, up_proj, mix_proj, down_proj, dw_kernel, gain1, gain2, stem, labels)

    pairs = [(c, s) for c in range(2) for s in range(2)]
    same = lax.ppermute(piece, ("core", "xh"), [(2 * c + s, 2 * s + c) for c, s in pairs])
    cross = lax.ppermute(piece, ("core", "xh"), [(2 * c + s, 2 * (1 - s) + c) for c, s in pairs])

    def both_ways(values, axes, ring):
        return lax.ppermute(values, axes, ring(1)), lax.ppermute(values, axes, ring(-1))

    near, away = both_ways(quarter, z_axes, z_ring)
    opposite = lax.ppermute(near, z_axes, z_ring(1))
    near, away, opposite, straight = lax.optimization_barrier((near, away, opposite, straight))
    quarters = pl.pallas_call(
        join_kernel,
        out_shape=shape(3 * QROWS, 2 * PAD1),
        in_specs=[WHOLE] * 3,
        out_specs=WHOLE,
        compiler_params=params(),
        name="join_quarters",
    )(near, away, opposite)
    straights = both_ways(straight, z_axes, z_ring)
    spread = both_ways(quarters, x_axes, x_ring)
    straights, spread, quarters, same, cross = lax.optimization_barrier((straights, spread, quarters, same, cross))
    mine = [
        *straights,
        lax.ppermute(straights[0], z_axes, z_ring(1)),
        quarters,
        *spread,
        lax.ppermute(spread[0], x_axes, x_ring(1)),
    ]
    weights = pl.pallas_call(
        columns_kernel,
        out_shape=tuple(shape(4, *dims, kind=BF16) for dims in weight_dims) + (shape(4, 8, 2 * PAD1),),
        in_specs=[SMEM] + [WHOLE] * 14 + [ANY] * 4,
        out_specs=(ANY,) * 4,
        scratch_shapes=[pltpu.VMEM((3,) + dims, BF16) for dims in weight_dims]
        + [pltpu.VMEM((3, 8, 2 * PAD1), F32), pltpu.VMEM((2, WROWS, 2 * PAD1), F32), pltpu.SemaphoreType.DMA((4, 4))],
        compiler_params=params(),
        name="columns",
    )(where, *mine, *[swap(part) for part in mine], up_proj, mix_proj, down_proj, aux)

    whole = pltpu.VMEM((192, PAD1), F32)

    def forward(halves, full):
        dims = [(192, PAD1) if full else (96, PAD1)]
        if full:
            dims += [(4, 128, C1), (4, 128, C1), (4, 32, C2)] + [(LROWS // 2, PAD1)] * 3 + [(LROWS, PAD1)]
        return pl.pallas_call(
            lambda *refs: forward_kernel(not halves, full, *refs),
            out_shape=tuple(shape(*each) for each in dims),
            in_specs=[SMEM] + [WHOLE] * (len(halves) + 6),
            out_specs=(WHOLE,) * len(dims),
            scratch_shapes=[pltpu.VMEM((LROWS, PAD1), F32)] * full + [pltpu.VMEM((128, PAD1), F32), whole],
            compiler_params=params(),
            name="forward_full" if full else "forward_light",
        )(where, *halves, same, cross, *weights)

    def hop(half, pairs):
        half = lax.ppermute(half, "y", pairs)
        return half, swap(half)

    arrived = [()]
    for tick in range(3):
        arrived.append(hop(forward(arrived[-1], False)[0], [(tick, tick + 1)]))
    msg, mixture, slope1, slope2, *lefts, left = forward(sum(arrived, ()), True)
    lefts = deliver(lefts)

    head = pl.pallas_call(
        head_kernel,
        out_shape=shape(192, PAD1),
        in_specs=[SMEM] + [WHOLE] * 6,
        out_specs=WHOLE,
        scratch_shapes=[pltpu.VMEM((128, HEAD), F32), pltpu.VMEM((32, HEAD), F32), pltpu.VMEM((128, PAD1), F32)],
        compiler_params=params(),
        name="head",
    )(where, msg, same, cross, lat_one, lat_two, classifier.T)

    def backward(halves, full):
        operands = [*halves, *([] if halves and not full else [head]), slope1, slope2, *weights]
        dims = [(96, PAD1)]
        if full:
            operands.append(mixture)
            dims = [(RROWS // 2 + 16, PAD1)] * 3 + [(RROWS, PAD1), (16, PAD1)]
        return pl.pallas_call(
            lambda *refs: backward_kernel(not halves, full, *refs),
            out_shape=tuple(shape(*each) for each in dims),
            in_specs=[SMEM] + [WHOLE] * len(operands),
            out_specs=(WHOLE,) * len(dims),
            scratch_shapes=[pltpu.VMEM((RROWS, PAD1), F32), pltpu.VMEM((128, C1), F32)] * full + [whole],
            compiler_params=params(),
            name="backward_full" if full else "backward_light",
        )(where, *operands)

    arrived = [()]
    for tick in range(3):
        arrived.append(hop(backward(arrived[-1], False)[0], [(3 - tick, 2 - tick)]))
        if tick == 1:
            arrived[-1], lefts = lax.optimization_barrier((arrived[-1], lefts))
            mates = [swap(part) for part in lefts]
        if tick == 2:
            arrived[-1], mates = lax.optimization_barrier((arrived[-1], mates))
    slots = backward(sum(arrived, ()), True)
    rights = deliver(slots[0:3])

    *partial, c0, c1, c2, c3 = pl.pallas_call(
        weight_kernel,
        out_shape=(shape(GROWS, PAD1),) * 4 + (shape(4, 4, PAD1),) * 4,
        in_specs=[SMEM] + [WHOLE] * 15,
        out_specs=(WHOLE,) * 8,
        scratch_shapes=[pltpu.VMEM((4, LROWS, PAD1), F32), pltpu.VMEM((4, RROWS, PAD1), F32)],
        compiler_params=params(),
        name="weight_grads",
    )(where, left, *lefts, *mates, slots[3], *rights, *[swap(part) for part in rights], slots[4])
    relay = lax.ppermute(partial[2], x_axes, x_ring(1))
    away = lax.ppermute(partial[1], x_axes, x_ring(-1))
    relay, away, cells = lax.optimization_barrier((relay, away, (c0, c1, c2, c3)))
    passed = pl.pallas_call(
        add_kernel,
        out_shape=shape(GROWS, PAD1),
        in_specs=[WHOLE] * 2,
        out_specs=WHOLE,
        compiler_params=params(),
        name="add_relay",
    )(partial[0], relay)
    near = lax.ppermute(passed, x_axes, x_ring(1))

    def stem_pairs(step):
        return [(4 * at + 2 * k + h, 4 * ((at + step) % 4) + 2 * h + k) for at in range(4) for k, h in pairs]

    cells = [lax.ppermute(cells[step], ("y", "core", "xh"), stem_pairs(step)) for step in range(4)]
    *grads, grad_stem = pl.pallas_call(
        final_kernel,
        out_shape=(shape(90, 1, C1), shape(45, 1, C1), shape(45, 1, C2), shape(9, 1, 45), shape(4, 2, 2, C1)),
        in_specs=[SMEM] + [WHOLE] * 7,
        out_specs=(WHOLE,) * 5,
        compiler_params=params(),
        name="final",
    )(where, partial[3], near, away, *cells)
    return (*[grad.transpose(1, 0, 2) for grad in grads], grad_stem)


def solution(mesh):
    fine = Mesh(mesh.devices.reshape(4, 4, 2, 2, 2), ("y", "z", "xl", "core", "xh"))
    col, dp, strip, both = ("y", "z"), ("xl", "core"), "xh", ("xl", "core", "xh")
    return jax.shard_map(
        shards,
        mesh=fine,
        in_specs=(
            P(dp, strip, None, None),
            P(dp, strip, None),
            P(col, None, None),
            P(col, None, None),
            P(col, None, None),
            P(col, None, None),
            P(col, None),
            P(col, None),
            P(),
            P(),
            P(),
        ),
        out_specs=(
            P(col, both, None),
            P(col, both, None),
            P(col, both, None),
            P(col, None, both),
            P(dp, strip, col, None),
        ),
        check_vma=False,
    )
```

```python
import jax
import jax.numpy as jnp
from jax import lax
from jax.experimental import pallas as pl
from jax.experimental.pallas import tpu as pltpu
from jax.sharding import Mesh, PartitionSpec as P

loss_scale = 64.0
root_coef = 0.7978845608028654
cube_coef = 0.044715

C1 = 360
C2 = 720
PAD1 = 384
HEAD = 512
CLASSES = 150
F32 = jnp.float32
BF16 = jnp.bfloat16
VMEM_LIMIT = 16 * 2**20
PACK_LIMIT = 60 * 2**20

WROWS = 464
QROWS = 64
AROWS = WROWS - 4 * QROWS
LROWS = 224
RROWS = 240
GROWS = 256


def params(limit=VMEM_LIMIT):
    return pltpu.CompilerParams(vmem_limit_bytes=limit)


def gelu_pair(values):
    inner = root_coef * (values + cube_coef * values * values * values)
    tangent = jnp.tanh(inner)
    result = 0.5 * values * (1.0 + tangent)
    slope = 0.5 * (1.0 + tangent) + 0.5 * values * (1.0 - tangent * tangent) * root_coef * (
        1.0 + 3.0 * cube_coef * values * values
    )
    return result, slope


def gelu_only(values):
    inner = root_coef * (values + cube_coef * values * values * values)
    return 0.5 * values * (1.0 + jnp.tanh(inner))


def dot(left, right):
    return jnp.dot(left, right, preferred_element_type=F32)


def dot_nt(left, right):
    return lax.dot_general(left, right, (((1,), (1,)), ((), ())), preferred_element_type=F32)


def dot_tn(left, right):
    return lax.dot_general(left, right, (((0,), (0,)), ((), ())), preferred_element_type=F32)


def shifted(even, odd):
    spot = lax.broadcasted_iota(jnp.int32, even.shape, 0)
    after = jnp.where(spot == 15, 0.0, pltpu.roll(even, 15, 0))
    before = jnp.where(spot == 0, 0.0, pltpu.roll(odd, 1, 0))
    return after, before


def neighbours(blocks):
    rows = []
    for r in range(4):
        even, odd = blocks[2 * r], blocks[2 * r + 1]
        after, before = shifted(even, odd)
        rows.append(((before, even, odd), (even, odd, after)))
    return rows


def stencil(rows, taps):
    out = []
    for r in range(4):
        for b in range(2):
            total = None
            for i in (-1, 0, 1):
                if 0 <= r + i < 4:
                    for j in range(3):
                        term = taps[3 * (i + 1) + j] * rows[r + i][b][j]
                        total = term if total is None else total + term
            out.append(total)
    return out


def tap_sums(rows, grads):
    sums = []
    for i in (-1, 0, 1):
        for j in range(3):
            total = None
            for r in range(4):
                if 0 <= r + i < 4:
                    for b in range(2):
                        term = rows[r + i][b][j] * grads[2 * r + b]
                        total = term if total is None else total + term
            sums.append(jnp.sum(total, axis=0, keepdims=True))
    return sums


def pool(blocks):
    parts = [blocks[4 * q] + blocks[4 * q + 1] + blocks[4 * q + 2] + blocks[4 * q + 3] for q in range(2)]
    return jnp.concatenate(parts, axis=0)


def split(values):
    return [values[16 * q : 16 * q + 16] for q in range(8)]


def join(blocks):
    return jnp.concatenate(blocks, axis=0)


def up2(values):
    return [values[16 * (q // 4) : 16 * (q // 4) + 16] for q in range(8)]


def decode_aux(aux):
    taps = [aux[t : t + 1, 0:C1] for t in range(8)] + [aux[0:1, PAD1 : PAD1 + C1]]
    gain1 = aux[1:2, PAD1 : PAD1 + C1]
    gain2 = jnp.concatenate([aux[2:3, PAD1 : 2 * PAD1], aux[3:4, PAD1:C2]], axis=1)
    return taps, gain1, gain2


def put(ref, row, values):
    width = values.shape[1]
    if width < PAD1:
        values = jnp.concatenate([values, jnp.zeros((values.shape[0], PAD1 - width), F32)], axis=1)
    ref[row : row + values.shape[0], :] = values


def put_two(ref, row, values):
    put(ref, row, values[:, 0:PAD1])
    put(ref, row + values.shape[0], values[:, PAD1:C2])


def get_two(ref, row):
    return jnp.concatenate([ref[row : row + 32, :], ref[row + 32 : row + 64, 0 : C2 - PAD1]], axis=1)


def pack_kernel(where, *refs):
    sources, outs, held, sems = refs[0:8], refs[8:12], refs[12:20], refs[22]
    (half_ref, wide_ref), (straight_ref, quarter_ref, piece_ref, aux_ref) = refs[20:22], outs
    up_ref, mix_ref, down_ref, tap_ref, g1_ref, g2_ref, stem_ref, label_ref = held
    core = where[2]
    copies = [
        pltpu.make_async_copy(src.at[where[1]] if at >= 6 else src, dst, sems.at[at])
        for at, (src, dst) in enumerate(zip(sources, held))
    ]
    for copy in copies:
        copy.start()
    for copy in copies:
        copy.wait()
    mix = mix_ref[0].astype(F32)
    taps = tap_ref[0].astype(F32)
    aux_ref[0:8, 0:C1] = taps[0:8]
    aux_ref[0:1, PAD1 : PAD1 + C1] = taps[8:9]
    aux_ref[1:2, PAD1 : PAD1 + C1] = g1_ref[...]
    aux_ref[2:3, PAD1 : 2 * PAD1] = g2_ref[:, 0:PAD1]
    aux_ref[3:4, PAD1:C2] = g2_ref[:, PAD1:C2]

    @pl.when(core == 0)
    def _():
        up = up_ref[0].astype(F32)
        half_ref[0:368, 0:C1] = up[0:368]
        half_ref[0:352, PAD1 : PAD1 + C1] = up[368:720]
        half_ref[368:464, 0:C1] = mix[0:96]
        half_ref[368:464, PAD1 : PAD1 + C1] = mix[96:192]

    @pl.when(core == 1)
    def _():
        half_ref[0:360, 0:C2] = down_ref[0].astype(F32)
        half_ref[360:368, :] = aux_ref[...]
        half_ref[368:464, 0:C1] = mix[192:288]
        half_ref[368:440, PAD1 : PAD1 + C1] = mix[288:360]

    straight_ref[...] = half_ref[0:AROWS, :]
    quarter_ref[...] = half_ref[pl.ds(pl.multiple_of(AROWS + where[3] * QROWS, 8), QROWS), :]

    wide = jnp.concatenate([stem_ref[...].astype(F32), jnp.zeros((2, 32, PAD1 - C1), F32)], axis=2)
    for part in range(3):
        wide_ref[part] = wide[:, :, 128 * part : 128 * part + 128]
    marks = label_ref[...].astype(F32)
    cell = lax.broadcasted_iota(jnp.int32, (16, 32), 0)
    pixel = lax.broadcasted_iota(jnp.int32, (16, 32), 1)
    lane = lax.broadcasted_iota(jnp.int32, (16, PAD1), 1)
    for a in range(2):
        for b in range(2):
            chosen = jnp.where(pixel == 2 * cell + b, marks[a : a + 1], 0.0)
            mark = jnp.sum(chosen, axis=1, keepdims=True)
            pixels = jnp.concatenate([wide_ref[part, a, pl.ds(b, 16, stride=2), :] for part in range(3)], axis=1)
            piece_ref[32 * a + 16 * b : 32 * a + 16 * b + 16, :] = jnp.where(lane == C1, mark, pixels)


def write_column(first, second, at, up_ref, mix_ref, down_ref, aux_ref):
    up = jnp.concatenate([first[0:368, 0:C1], first[0:352, PAD1 : PAD1 + C1]], axis=0)
    up_ref[at] = up.astype(BF16)
    mix = jnp.concatenate(
        [
            first[368:464, 0:C1],
            first[368:464, PAD1 : PAD1 + C1],
            second[368:464, 0:C1],
            second[368:440, PAD1 : PAD1 + C1],
        ],
        axis=0,
    )
    mix_ref[at] = mix.astype(BF16)
    down_ref[at] = second[0:360, 0:C2].astype(BF16)
    aux_ref[at] = second[360:368, :]


def join_kernel(first, second, third, out_ref):
    for at, ref in enumerate((first, second, third)):
        out_ref[QROWS * at : QROWS * at + QROWS, :] = ref[...]


def add_kernel(first, second, out_ref):
    out_ref[...] = first[...] + second[...]


def columns_kernel(where, *refs):
    mine, theirs, own, refs = refs[0:7], refs[7:14], refs[14:18], refs[18:]
    outs, parts, halves, sems = refs[0:4], refs[4:8], refs[8], refs[9]
    core, spot = where[2], where[3]
    sign = 1 - 2 * core

    def moves(at):
        if at == 3:
            sources = [ref.at[0] for ref in own[0:3]] + [own[3]]
            column = where[1]
        else:
            sources = [ref.at[at] for ref in parts]
            column = lax.rem(where[1] + 4 - sign * (1, -1, 2)[at], 4)
        return [pltpu.make_async_copy(src, outs[k].at[column], sems.at[at, k]) for k, src in enumerate(sources)]

    for move in moves(3):
        move.start()
    for at in range(3):
        for pieces, hand, place, which in ((mine, sign, core, at), (theirs, -sign, 1 - core, (1, 0, 2)[at])):
            halves[place, 0:AROWS, :] = pieces[which][...]
            for quarters, shift in zip(pieces[3:7], (0, 1, -1, 2)):
                source = lax.rem(spot + 4 - hand * shift, 4)
                rows = pl.ds(pl.multiple_of(AROWS + source * QROWS, 8), QROWS)
                halves[place, rows, :] = quarters[QROWS * which : QROWS * which + QROWS, :]
        write_column(halves.at[0], halves.at[1], at, *parts)
        for move in moves(at):
            move.start()
    for at in range(4):
        for move in moves(at):
            move.wait()


def hand_over(where, column, factors, slots):
    half = factors.shape[0] // 2
    for at in range(3):

        @pl.when(column == where[4 + at])
        def _(at=at):
            slots[at][0:half, :] = factors[pl.ds(pl.multiple_of(where[2] * half, 8), half), :]

    @pl.when(column == where[1])
    def _():
        slots[3][...] = factors[...]


def take(where, halves, whole):
    core = where[2]
    whole[pl.ds(pl.multiple_of(core * 96, 8), 96), :] = halves[0][...]
    whole[pl.ds(pl.multiple_of((1 - core) * 96, 8), 96), :] = halves[1][...]


def take_own(where, pairs, planes, start, whole):
    for at, plane in enumerate(planes):

        @pl.when(where[0] == plane)
        def _(at=at):
            take(where, pairs[2 * at : 2 * at + 2], whole)

    @pl.when(where[0] == 6 - sum(planes))
    def _():
        whole[...] = jnp.zeros((192, PAD1), F32) if start is None else start[...]


def unfold(whole):
    return whole[0:128, 0:C1], get_two(whole, 128)


def give(where, first, second, whole, half):
    put(whole, 0, first)
    put_two(whole, 128, second)
    half[...] = whole[pl.ds(pl.multiple_of(where[2] * 96, 8), 96), :]


def read_crop(where, same, cross, crop):
    crop[pl.ds(pl.multiple_of(where[2] * 64, 8), 64), :] = same[...]
    crop[pl.ds(pl.multiple_of((1 - where[2]) * 64, 8), 64), :] = cross[...]


def forward_kernel(opening, full, where, *refs):
    if opening:
        state1, state2 = jnp.zeros((128, C1), F32), jnp.zeros((32, C2), F32)
    elif full:
        take_own(where, refs[0:6], (1, 2, 3), None, refs[-1])
        state1, state2 = unfold(refs[-1])
        refs = refs[6:]
    else:
        take(where, refs[0:2], refs[-1])
        state1, state2 = unfold(refs[-1])
        refs = refs[2:]
    same_ref, cross_ref, up_ref, mix_ref, down_ref, aux_ref, out_ref, *rest = refs
    crop_ref, whole = refs[-2:]
    read_crop(where, same_ref, cross_ref, crop_ref)
    if full:
        mixture_ref, slope1_ref, slope2_ref, *slots = rest[:-3]
        factors = rest[-3]
    for column in range(4):
        taps, gain1, gain2 = decode_aux(aux_ref[column])
        narrow = state2.astype(BF16)
        ups = up2(dot(narrow, up_ref[column]))
        mixture = [crop_ref[16 * q : 16 * q + 16, 0:C1] + ups[q] for q in range(8)]
        depth = join(stencil(neighbours(mixture), taps))
        if full:
            active, slope1 = gelu_pair(depth)
        else:
            active = gelu_only(depth)
        hidden = active.astype(BF16)
        state1 = gain1 * state1 + dot(hidden, mix_ref[column])
        pooled = (pool(split(state1)) * 0.25).astype(BF16)
        lifted = dot(pooled, down_ref[column])
        if full:
            active2, slope2 = gelu_pair(lifted)
        else:
            active2 = gelu_only(lifted)
        state2 = gain2 * state2 + active2
        if full:
            mixture_ref[column] = join(mixture)
            slope1_ref[column] = slope1
            slope2_ref[column] = slope2
            put(factors, 0, hidden.astype(F32))
            put(factors, 128, pooled.astype(F32))
            put_two(factors, 160, narrow.astype(F32))
            hand_over(where, column, factors, slots)
    if full:
        put(out_ref, 0, state1)
        put_two(out_ref, 128, state2)
    else:
        give(where, state1, state2, whole, out_ref)


def head_kernel(where, msg_ref, same_ref, cross_ref, one_ref, two_ref, cls_ref, out_ref, first, second, crop_ref):
    read_crop(where, same_ref, cross_ref, crop_ref)
    state1 = msg_ref[0:128, 0:C1].astype(BF16)
    state2 = get_two(msg_ref, 128).astype(BF16)
    labels = crop_ref[:, C1 : C1 + 1].astype(jnp.int32)
    second[...] = dot(state2, two_ref[...])
    first[...] = dot(state1, one_ref[...])
    lateral = first[...] + join(up2(second[...]))
    active, slope = gelu_pair(lateral)
    logits = dot_nt(active.astype(BF16), cls_ref[...])
    classes = lax.broadcasted_iota(jnp.int32, logits.shape, 1)
    logits = logits - jnp.max(logits, axis=-1, keepdims=True)
    powers = jnp.exp(logits)
    probs = powers / jnp.sum(powers, axis=-1, keepdims=True)
    onehot = (classes == labels).astype(F32)
    grad_logits = (probs - onehot) * (loss_scale / 2048.0)
    grad_lat = dot(grad_logits.astype(BF16), cls_ref[...]) * slope
    put(out_ref, 0, dot_nt(grad_lat.astype(BF16), one_ref[...]))
    put_two(out_ref, 128, dot_nt(pool(split(grad_lat)).astype(BF16), two_ref[...]))


def backward_kernel(opening, full, where, *refs):
    if opening:
        head_ref, *refs = refs
        cot1, cot2 = unfold(head_ref)
    elif full:
        take_own(where, refs[0:6], (2, 1, 0), refs[6], refs[-1])
        cot1, cot2 = unfold(refs[-1])
        refs = refs[7:]
    else:
        take(where, refs[0:2], refs[-1])
        cot1, cot2 = unfold(refs[-1])
        refs = refs[2:]
    slope1_ref, slope2_ref, up_ref, mix_ref, down_ref, aux_ref, *rest = refs
    if full:
        mixture_ref, *slots, stem_own, factors, stem_sum, whole = rest
    else:
        out_ref, whole = rest
    for column in (3, 2, 1, 0):
        taps, gain1, gain2 = decode_aux(aux_ref[column])
        grad_s = (cot2 * slope2_ref[column]).astype(BF16)
        back = dot_nt(grad_s, down_ref[column]) * 0.25
        total1 = cot1 + join(up2(back))
        narrow_total = total1.astype(BF16)
        grad_depth = dot_nt(narrow_total, mix_ref[column]) * slope1_ref[column]
        grads = split(grad_depth)
        grad_mixture = stencil(neighbours(grads), taps[::-1])
        grad_narrow = pool(grad_mixture).astype(BF16)
        if not full or column > 0:
            cot2 = gain2 * cot2 + dot_nt(grad_narrow, up_ref[column])
            cot1 = gain1 * total1
        if full:
            put(factors, 0, narrow_total.astype(F32))
            put(factors, 128, grad_narrow.astype(F32))
            put_two(factors, 160, grad_s.astype(F32))
            sums = tap_sums(neighbours(split(mixture_ref[column])), grads)
            put(factors, 224, jnp.concatenate(sums + [jnp.zeros((7, C1), F32)], axis=0))
            hand_over(where, column, factors, slots)
            mixed = join(grad_mixture)
            stem_sum[...] = mixed if column == 3 else stem_sum[...] + mixed
    if full:
        mine = stem_sum[pl.ds(pl.multiple_of(where[2] * 64, 8), 64), :]
        mine = jnp.concatenate([mine, jnp.zeros((64, PAD1 - C1), F32)], axis=1)
        targets = [(where[4 + at], slots[at].at[RROWS // 2 :]) for at in range(3)] + [(where[1], stem_own)]
        for cell in range(4):
            rows = [16 * q + 4 * y + cell for y in range(4) for q in range(4)]
            part = join([mine[row : row + 1] for row in rows])
            for target, ref in targets:

                @pl.when(target == cell)
                def _(part=part, ref=ref):
                    ref[...] = part
    else:
        give(where, cot1, cot2, whole, out_ref)


def weight_kernel(where, lo, l1, l2, l3, m1, m2, m3, ro, r1, r2, r3, s1, s2, s3, stem_own, *rest):
    *outs, c0, c1, c2, c3, left, right = rest
    core = where[2]
    for full_ref, own, pairs, rows in (
        (left, lo, ((l1, m2), (l2, m1), (l3, m3)), LROWS),
        (right, ro, ((r1, s2), (r2, s1), (r3, s3)), RROWS),
    ):
        half = rows // 2
        mine = pl.ds(pl.multiple_of(core * half, 8), half)
        other = pl.ds(pl.multiple_of((1 - core) * half, 8), half)
        full_ref[0] = own[...]
        for at, (near, far) in enumerate(pairs):
            full_ref[at + 1, mine, :] = near[0:half, :]
            full_ref[at + 1, other, :] = far[0:half, :]

    def stack(ref, row, count):
        return jnp.concatenate([ref[q, row : row + count, :] for q in range(4)], axis=0)

    hidden = stack(left, 0, 128)
    pooled = stack(left, 128, 32)
    narrow = jnp.concatenate([stack(left, 160, 32), stack(left, 192, 32)], axis=1)
    total = stack(right, 0, 128).astype(BF16)
    grad_narrow = stack(right, 128, 32).astype(BF16)
    grad_lo = stack(right, 160, 32).astype(BF16)
    grad_hi = stack(right, 192, 32).astype(BF16)
    taps = right[0, 224:240, :] + right[1, 224:240, :] + right[2, 224:240, :] + right[3, 224:240, :]
    for at, out_ref in enumerate(outs):
        block = where[7 + at]
        back1 = lax.rem(PAD1 - 45 * block, PAD1)
        back2 = lax.rem(2 * PAD1 - 90 * block, 2 * PAD1)
        some_hidden = pltpu.roll(hidden, back1, 1)[:, 0:128].astype(BF16)
        some_pooled = pltpu.roll(pooled, back1, 1)[:, 0:128].astype(BF16)
        some_narrow = pltpu.roll(narrow, back2, 1)[:, 0:128].astype(BF16)
        out_ref[0:96, :] = dot_tn(some_narrow, grad_narrow)[0:96]
        out_ref[96:144, :] = dot_tn(some_hidden, total)[0:48]
        out_ref[144:192, :] = dot_tn(some_pooled, grad_lo)[0:48]
        out_ref[192:240, :] = dot_tn(some_pooled, grad_hi)[0:48]
        out_ref[240:256, :] = pltpu.roll(taps, back1, 1)
    z, sign, skip = where[1], 1 - 2 * core, RROWS // 2
    sources = ((stem_own, 0, z), (r1, skip, z - sign), (r2, skip, z + sign), (r3, skip, z + 2))
    for ref, row, source in sources:
        for cell in range(4):
            part = ref[row + 4 * cell : row + 4 * cell + 4, :]
            for shift, out_ref in enumerate((c0, c1, c2, c3)):

                @pl.when(lax.rem(where[0] + shift, 4) == cell)
                def _(part=part, out_ref=out_ref, source=source):
                    out_ref[lax.rem(source + 4, 4)] = part


def final_kernel(where, own, near, far, c0, c1, c2, c3, up_ref, mix_ref, down_ref, tap_ref, stem_ref):
    total = own[...] + near[...] + far[...]
    up_ref[:, 0, :] = total[0:90, 0:C1]
    mix_ref[:, 0, :] = total[96:141, 0:C1]
    down_ref[:, 0, 0:PAD1] = total[144:189]
    down_ref[:, 0, PAD1:C2] = total[192:237, 0 : C2 - PAD1]
    tap_ref[:, 0, :] = total[240:249, 0:45]
    cells = c0[...] + c1[...] + c2[...] + c3[...]
    stem_ref[:, 0] = cells[:, 0:2, 0:C1]
    stem_ref[:, 1] = cells[:, 2:4, 0:C1]


def shape(*dims, kind=F32):
    return jax.ShapeDtypeStruct(dims, kind)


SMEM = pl.BlockSpec(memory_space=pltpu.SMEM)
WHOLE = pl.BlockSpec(memory_space=pltpu.VMEM)
ANY = pl.BlockSpec(memory_space=pl.ANY)
HBM = pl.BlockSpec(memory_space=pltpu.HBM)


def shards(stem, labels, up_proj, mix_proj, down_proj, dw_kernel, gain1, gain2, lat_one, lat_two, classifier):
    y, z = lax.axis_index("y"), lax.axis_index("z")
    core = lax.axis_index("core")
    sign = 1 - 2 * core
    spot = lax.axis_index("xh") * 2 + lax.axis_index("xl")

    def around(at):
        return [(at + sign + 4) % 4, (at - sign + 4) % 4, (at + 2) % 4]

    blocks = [(x % 2) * 4 + core * 2 + x // 2 for x in around(spot) + [spot]]
    where = jnp.stack([y, z, core, spot, *around(z), *blocks]).astype(jnp.int32)

    def z_ring(step):
        return [
            (2 * at + c, 2 * ((at + (step if c == 0 else -step)) % 4) + c) for at in range(4) for c in range(2)
        ]

    def x_spot(x, c):
        return ((x % 2) * 2 + c) * 2 + x // 2

    def x_ring(step):
        return [
            (x_spot(x, c), x_spot((x + (step if c == 0 else -step)) % 4, c)) for x in range(4) for c in range(2)
        ]

    z_axes, x_axes = ("z", "core"), ("xl", "core", "xh")

    def swap(values):
        return lax.ppermute(values, "core", [(0, 1), (1, 0)])

    def deliver(slots):
        near = lax.ppermute(slots[0], z_axes, z_ring(1))
        away = lax.ppermute(slots[1], z_axes, z_ring(-1))
        opposite = lax.ppermute(slots[2], z_axes, z_ring(2))
        return near, away, opposite

    weight_dims = ((C2, C1), (C1, C1), (C1, C2))
    straight, quarter, piece, aux = pl.pallas_call(
        pack_kernel,
        out_shape=(shape(AROWS, 2 * PAD1), shape(QROWS, 2 * PAD1), shape(64, PAD1), shape(8, 2 * PAD1)),
        in_specs=[SMEM] + [HBM] * 8,
        out_specs=(WHOLE,) * 4,
        scratch_shapes=[pltpu.VMEM((1,) + dims, BF16) for dims in weight_dims]
        + [pltpu.VMEM((1, 9, C1), BF16), pltpu.VMEM((1, C1), F32), pltpu.VMEM((1, C2), F32)]
        + [pltpu.VMEM((2, 32, C1), BF16), pltpu.VMEM((2, 32), jnp.int32)]
        + [pltpu.VMEM((WROWS, 2 * PAD1), F32), pltpu.VMEM((3, 2, 32, 128), F32), pltpu.SemaphoreType.DMA((8,))],
        compiler_params=params(PACK_LIMIT),
        name="pack",
    )(where, up_proj, mix_proj, down_proj, dw_kernel, gain1, gain2, stem, labels)

    pairs = [(c, s) for c in range(2) for s in range(2)]
    same = lax.ppermute(piece, ("core", "xh"), [(2 * c + s, 2 * s + c) for c, s in pairs])
    cross = lax.ppermute(piece, ("core", "xh"), [(2 * c + s, 2 * (1 - s) + c) for c, s in pairs])

    def both_ways(values, axes, ring):
        return lax.ppermute(values, axes, ring(1)), lax.ppermute(values, axes, ring(-1))

    near, away = both_ways(quarter, z_axes, z_ring)
    near, away, same, cross = lax.optimization_barrier((near, away, same, cross))
    opposite = lax.ppermute(near, z_axes, z_ring(1))
    opposite, straight = lax.optimization_barrier((opposite, straight))
    quarters = pl.pallas_call(
        join_kernel,
        out_shape=shape(3 * QROWS, 2 * PAD1),
        in_specs=[WHOLE] * 3,
        out_specs=WHOLE,
        compiler_params=params(),
        name="join_quarters",
    )(near, away, opposite)
    straights = both_ways(straight, z_axes, z_ring)
    spread = both_ways(quarters, x_axes, x_ring)
    straights, spread, quarters = lax.optimization_barrier((straights, spread, quarters))
    mine = [
        *straights,
        lax.ppermute(straights[0], z_axes, z_ring(1)),
        quarters,
        *spread,
        lax.ppermute(spread[0], x_axes, x_ring(1)),
    ]
    weights = pl.pallas_call(
        columns_kernel,
        out_shape=tuple(shape(4, *dims, kind=BF16) for dims in weight_dims) + (shape(4, 8, 2 * PAD1),),
        in_specs=[SMEM] + [WHOLE] * 14 + [ANY] * 4,
        out_specs=(ANY,) * 4,
        scratch_shapes=[pltpu.VMEM((3,) + dims, BF16) for dims in weight_dims]
        + [pltpu.VMEM((3, 8, 2 * PAD1), F32), pltpu.VMEM((2, WROWS, 2 * PAD1), F32), pltpu.SemaphoreType.DMA((4, 4))],
        compiler_params=params(),
        name="columns",
    )(where, *mine, *[swap(part) for part in mine], up_proj, mix_proj, down_proj, aux)

    whole = pltpu.VMEM((192, PAD1), F32)

    def forward(halves, full):
        dims = [(192, PAD1) if full else (96, PAD1)]
        if full:
            dims += [(4, 128, C1), (4, 128, C1), (4, 32, C2)] + [(LROWS // 2, PAD1)] * 3 + [(LROWS, PAD1)]
        return pl.pallas_call(
            lambda *refs: forward_kernel(not halves, full, *refs),
            out_shape=tuple(shape(*each) for each in dims),
            in_specs=[SMEM] + [WHOLE] * (len(halves) + 6),
            out_specs=(WHOLE,) * len(dims),
            scratch_shapes=[pltpu.VMEM((LROWS, PAD1), F32)] * full + [pltpu.VMEM((128, PAD1), F32), whole],
            compiler_params=params(),
            name="forward_full" if full else "forward_light",
        )(where, *halves, same, cross, *weights)

    def hop(half, pairs):
        half = lax.ppermute(half, "y", pairs)
        return half, swap(half)

    arrived = [()]
    for tick in range(3):
        arrived.append(hop(forward(arrived[-1], False)[0], [(tick, tick + 1)]))
    msg, mixture, slope1, slope2, *lefts, left = forward(sum(arrived, ()), True)
    lefts = deliver(lefts)

    head = pl.pallas_call(
        head_kernel,
        out_shape=shape(192, PAD1),
        in_specs=[SMEM] + [WHOLE] * 6,
        out_specs=WHOLE,
        scratch_shapes=[pltpu.VMEM((128, HEAD), F32), pltpu.VMEM((32, HEAD), F32), pltpu.VMEM((128, PAD1), F32)],
        compiler_params=params(),
        name="head",
    )(where, msg, same, cross, lat_one, lat_two, classifier.T)

    def backward(halves, full):
        operands = [*halves, *([] if halves and not full else [head]), slope1, slope2, *weights]
        dims = [(96, PAD1)]
        if full:
            operands.append(mixture)
            dims = [(RROWS // 2 + 16, PAD1)] * 3 + [(RROWS, PAD1), (16, PAD1)]
        return pl.pallas_call(
            lambda *refs: backward_kernel(not halves, full, *refs),
            out_shape=tuple(shape(*each) for each in dims),
            in_specs=[SMEM] + [WHOLE] * len(operands),
            out_specs=(WHOLE,) * len(dims),
            scratch_shapes=[pltpu.VMEM((RROWS, PAD1), F32), pltpu.VMEM((128, C1), F32)] * full + [whole],
            compiler_params=params(),
            name="backward_full" if full else "backward_light",
        )(where, *operands)

    arrived = [()]
    for tick in range(3):
        arrived.append(hop(backward(arrived[-1], False)[0], [(3 - tick, 2 - tick)]))
        if tick == 1:
            arrived[-1], lefts = lax.optimization_barrier((arrived[-1], lefts))
            mates = [swap(part) for part in lefts]
        if tick == 2:
            arrived[-1], mates = lax.optimization_barrier((arrived[-1], mates))
    slots = backward(sum(arrived, ()), True)
    rights = deliver(slots[0:3])

    *partial, c0, c1, c2, c3 = pl.pallas_call(
        weight_kernel,
        out_shape=(shape(GROWS, PAD1),) * 4 + (shape(4, 4, PAD1),) * 4,
        in_specs=[SMEM] + [WHOLE] * 15,
        out_specs=(WHOLE,) * 8,
        scratch_shapes=[pltpu.VMEM((4, LROWS, PAD1), F32), pltpu.VMEM((4, RROWS, PAD1), F32)],
        compiler_params=params(),
        name="weight_grads",
    )(where, left, *lefts, *mates, slots[3], *rights, *[swap(part) for part in rights], slots[4])
    relay = lax.ppermute(partial[2], x_axes, x_ring(1))
    away = lax.ppermute(partial[1], x_axes, x_ring(-1))
    relay, away, cells = lax.optimization_barrier((relay, away, (c0, c1, c2, c3)))
    passed = pl.pallas_call(
        add_kernel,
        out_shape=shape(GROWS, PAD1),
        in_specs=[WHOLE] * 2,
        out_specs=WHOLE,
        compiler_params=params(),
        name="add_relay",
    )(partial[0], relay)
    near = lax.ppermute(passed, x_axes, x_ring(1))

    def stem_pairs(step):
        return [(4 * at + 2 * k + h, 4 * ((at + step) % 4) + 2 * h + k) for at in range(4) for k, h in pairs]

    cells = [lax.ppermute(cells[step], ("y", "core", "xh"), stem_pairs(step)) for step in range(4)]
    *grads, grad_stem = pl.pallas_call(
        final_kernel,
        out_shape=(shape(90, 1, C1), shape(45, 1, C1), shape(45, 1, C2), shape(9, 1, 45), shape(4, 2, 2, C1)),
        in_specs=[SMEM] + [WHOLE] * 7,
        out_specs=(WHOLE,) * 5,
        compiler_params=params(),
        name="final",
    )(where, partial[3], near, away, *cells)
    return (*[grad.transpose(1, 0, 2) for grad in grads], grad_stem)


def solution(mesh):
    fine = Mesh(mesh.devices.reshape(4, 4, 2, 2, 2), ("y", "z", "xl", "core", "xh"))
    col, dp, strip, both = ("y", "z"), ("xl", "core"), "xh", ("xl", "core", "xh")
    return jax.shard_map(
        shards,
        mesh=fine,
        in_specs=(
            P(dp, strip, None, None),
            P(dp, strip, None),
            P(col, None, None),
            P(col, None, None),
            P(col, None, None),
            P(col, None, None),
            P(col, None),
            P(col, None),
            P(),
            P(),
            P(),
        ),
        out_specs=(
            P(col, both, None),
            P(col, both, None),
            P(col, both, None),
            P(col, None, both),
            P(dp, strip, col, None),
        ),
        check_vma=False,
    )
```

```python
import jax
import jax.numpy as jnp
from jax import lax
from jax.experimental import pallas as pl
from jax.experimental.pallas import tpu as pltpu
from jax.sharding import Mesh, PartitionSpec as P

loss_scale = 64.0
root_coef = 0.7978845608028654
cube_coef = 0.044715

C1 = 360
C2 = 720
PAD1 = 384
HEAD = 512
CLASSES = 150
F32 = jnp.float32
BF16 = jnp.bfloat16
VMEM_LIMIT = 16 * 2**20
PACK_LIMIT = 60 * 2**20

WROWS = 464
QROWS = 64
AROWS = WROWS - 4 * QROWS
LROWS = 224
RROWS = 240
GROWS = 256


def params(limit=VMEM_LIMIT):
    return pltpu.CompilerParams(vmem_limit_bytes=limit)


def gelu_pair(values):
    inner = root_coef * (values + cube_coef * values * values * values)
    tangent = jnp.tanh(inner)
    result = 0.5 * values * (1.0 + tangent)
    slope = 0.5 * (1.0 + tangent) + 0.5 * values * (1.0 - tangent * tangent) * root_coef * (
        1.0 + 3.0 * cube_coef * values * values
    )
    return result, slope


def gelu_only(values):
    inner = root_coef * (values + cube_coef * values * values * values)
    return 0.5 * values * (1.0 + jnp.tanh(inner))


def dot(left, right):
    return jnp.dot(left, right, preferred_element_type=F32)


def dot_nt(left, right):
    return lax.dot_general(left, right, (((1,), (1,)), ((), ())), preferred_element_type=F32)


def dot_tn(left, right):
    return lax.dot_general(left, right, (((0,), (0,)), ((), ())), preferred_element_type=F32)


def shifted(even, odd):
    spot = lax.broadcasted_iota(jnp.int32, even.shape, 0)
    after = jnp.where(spot == 15, 0.0, pltpu.roll(even, 15, 0))
    before = jnp.where(spot == 0, 0.0, pltpu.roll(odd, 1, 0))
    return after, before


def neighbours(blocks):
    rows = []
    for r in range(4):
        even, odd = blocks[2 * r], blocks[2 * r + 1]
        after, before = shifted(even, odd)
        rows.append(((before, even, odd), (even, odd, after)))
    return rows


def stencil(rows, taps):
    out = []
    for r in range(4):
        for b in range(2):
            total = None
            for i in (-1, 0, 1):
                if 0 <= r + i < 4:
                    for j in range(3):
                        term = taps[3 * (i + 1) + j] * rows[r + i][b][j]
                        total = term if total is None else total + term
            out.append(total)
    return out


def tap_sums(rows, grads):
    sums = []
    for i in (-1, 0, 1):
        for j in range(3):
            total = None
            for r in range(4):
                if 0 <= r + i < 4:
                    for b in range(2):
                        term = rows[r + i][b][j] * grads[2 * r + b]
                        total = term if total is None else total + term
            sums.append(jnp.sum(total, axis=0, keepdims=True))
    return sums


def pool(blocks):
    parts = [blocks[4 * q] + blocks[4 * q + 1] + blocks[4 * q + 2] + blocks[4 * q + 3] for q in range(2)]
    return jnp.concatenate(parts, axis=0)


def split(values):
    return [values[16 * q : 16 * q + 16] for q in range(8)]


def join(blocks):
    return jnp.concatenate(blocks, axis=0)


def up2(values):
    return [values[16 * (q // 4) : 16 * (q // 4) + 16] for q in range(8)]


def decode_aux(aux):
    taps = [aux[t : t + 1, 0:C1] for t in range(8)] + [aux[0:1, PAD1 : PAD1 + C1]]
    gain1 = aux[1:2, PAD1 : PAD1 + C1]
    gain2 = jnp.concatenate([aux[2:3, PAD1 : 2 * PAD1], aux[3:4, PAD1:C2]], axis=1)
    return taps, gain1, gain2


def put(ref, row, values):
    width = values.shape[1]
    if width < PAD1:
        values = jnp.concatenate([values, jnp.zeros((values.shape[0], PAD1 - width), F32)], axis=1)
    ref[row : row + values.shape[0], :] = values


def put_two(ref, row, values):
    put(ref, row, values[:, 0:PAD1])
    put(ref, row + values.shape[0], values[:, PAD1:C2])


def get_two(ref, row):
    return jnp.concatenate([ref[row : row + 32, :], ref[row + 32 : row + 64, 0 : C2 - PAD1]], axis=1)


def pack_kernel(where, *refs):
    sources, outs, held, sems = refs[0:8], refs[8:12], refs[12:20], refs[22]
    (half_ref, wide_ref), (straight_ref, quarter_ref, piece_ref, aux_ref) = refs[20:22], outs
    up_ref, mix_ref, down_ref, tap_ref, g1_ref, g2_ref, stem_ref, label_ref = held
    core = where[2]
    copies = [
        pltpu.make_async_copy(src.at[where[1]] if at >= 6 else src, dst, sems.at[at])
        for at, (src, dst) in enumerate(zip(sources, held))
    ]
    for copy in copies:
        copy.start()
    for copy in copies:
        copy.wait()
    mix = mix_ref[0].astype(F32)
    taps = tap_ref[0].astype(F32)
    aux_ref[0:8, 0:C1] = taps[0:8]
    aux_ref[0:1, PAD1 : PAD1 + C1] = taps[8:9]
    aux_ref[1:2, PAD1 : PAD1 + C1] = g1_ref[...]
    aux_ref[2:3, PAD1 : 2 * PAD1] = g2_ref[:, 0:PAD1]
    aux_ref[3:4, PAD1:C2] = g2_ref[:, PAD1:C2]

    @pl.when(core == 0)
    def _():
        up = up_ref[0].astype(F32)
        half_ref[0:368, 0:C1] = up[0:368]
        half_ref[0:352, PAD1 : PAD1 + C1] = up[368:720]
        half_ref[368:464, 0:C1] = mix[0:96]
        half_ref[368:464, PAD1 : PAD1 + C1] = mix[96:192]

    @pl.when(core == 1)
    def _():
        half_ref[0:360, 0:C2] = down_ref[0].astype(F32)
        half_ref[360:368, :] = aux_ref[...]
        half_ref[368:464, 0:C1] = mix[192:288]
        half_ref[368:440, PAD1 : PAD1 + C1] = mix[288:360]

    straight_ref[...] = half_ref[0:AROWS, :]
    quarter_ref[...] = half_ref[pl.ds(pl.multiple_of(AROWS + where[3] * QROWS, 8), QROWS), :]

    wide = jnp.concatenate([stem_ref[...].astype(F32), jnp.zeros((2, 32, PAD1 - C1), F32)], axis=2)
    for part in range(3):
        wide_ref[part] = wide[:, :, 128 * part : 128 * part + 128]
    marks = label_ref[...].astype(F32)
    cell = lax.broadcasted_iota(jnp.int32, (16, 32), 0)
    pixel = lax.broadcasted_iota(jnp.int32, (16, 32), 1)
    lane = lax.broadcasted_iota(jnp.int32, (16, PAD1), 1)
    for a in range(2):
        for b in range(2):
            chosen = jnp.where(pixel == 2 * cell + b, marks[a : a + 1], 0.0)
            mark = jnp.sum(chosen, axis=1, keepdims=True)
            pixels = jnp.concatenate([wide_ref[part, a, pl.ds(b, 16, stride=2), :] for part in range(3)], axis=1)
            piece_ref[32 * a + 16 * b : 32 * a + 16 * b + 16, :] = jnp.where(lane == C1, mark, pixels)


def write_column(first, second, at, up_ref, mix_ref, down_ref, aux_ref):
    up = jnp.concatenate([first[0:368, 0:C1], first[0:352, PAD1 : PAD1 + C1]], axis=0)
    up_ref[at] = up.astype(BF16)
    mix = jnp.concatenate(
        [
            first[368:464, 0:C1],
            first[368:464, PAD1 : PAD1 + C1],
            second[368:464, 0:C1],
            second[368:440, PAD1 : PAD1 + C1],
        ],
        axis=0,
    )
    mix_ref[at] = mix.astype(BF16)
    down_ref[at] = second[0:360, 0:C2].astype(BF16)
    aux_ref[at] = second[360:368, :]


def join_kernel(first, second, third, out_ref):
    for at, ref in enumerate((first, second, third)):
        out_ref[QROWS * at : QROWS * at + QROWS, :] = ref[...]


def add_kernel(first, second, out_ref):
    out_ref[...] = first[...] + second[...]


def columns_kernel(where, *refs):
    mine, theirs, own, refs = refs[0:7], refs[7:14], refs[14:18], refs[18:]
    outs, parts, halves, sems = refs[0:4], refs[4:8], refs[8], refs[9]
    core, spot = where[2], where[3]
    sign = 1 - 2 * core

    def moves(at):
        if at == 3:
            sources = [ref.at[0] for ref in own[0:3]] + [own[3]]
            column = where[1]
        else:
            sources = [ref.at[at] for ref in parts]
            column = lax.rem(where[1] + 4 - sign * (1, -1, 2)[at], 4)
        return [pltpu.make_async_copy(src, outs[k].at[column], sems.at[at, k]) for k, src in enumerate(sources)]

    for move in moves(3):
        move.start()
    for at in range(3):
        for pieces, hand, place, which in ((mine, sign, core, at), (theirs, -sign, 1 - core, (1, 0, 2)[at])):
            halves[place, 0:AROWS, :] = pieces[which][...]
            for quarters, shift in zip(pieces[3:7], (0, 1, -1, 2)):
                source = lax.rem(spot + 4 - hand * shift, 4)
                rows = pl.ds(pl.multiple_of(AROWS + source * QROWS, 8), QROWS)
                halves[place, rows, :] = quarters[QROWS * which : QROWS * which + QROWS, :]
        write_column(halves.at[0], halves.at[1], at, *parts)
        for move in moves(at):
            move.start()
    for at in range(4):
        for move in moves(at):
            move.wait()


def hand_over(where, column, factors, slots):
    half = factors.shape[0] // 2
    for at in range(3):

        @pl.when(column == where[4 + at])
        def _(at=at):
            slots[at][0:half, :] = factors[pl.ds(pl.multiple_of(where[2] * half, 8), half), :]

    @pl.when(column == where[1])
    def _():
        slots[3][...] = factors[...]


def take(where, halves, whole):
    core = where[2]
    whole[pl.ds(pl.multiple_of(core * 96, 8), 96), :] = halves[0][...]
    whole[pl.ds(pl.multiple_of((1 - core) * 96, 8), 96), :] = halves[1][...]


def take_own(where, pairs, planes, start, whole):
    for at, plane in enumerate(planes):

        @pl.when(where[0] == plane)
        def _(at=at):
            take(where, pairs[2 * at : 2 * at + 2], whole)

    @pl.when(where[0] == 6 - sum(planes))
    def _():
        whole[...] = jnp.zeros((192, PAD1), F32) if start is None else start[...]


def unfold(whole):
    return whole[0:128, 0:C1], get_two(whole, 128)


def give(where, first, second, whole, half):
    put(whole, 0, first)
    put_two(whole, 128, second)
    half[...] = whole[pl.ds(pl.multiple_of(where[2] * 96, 8), 96), :]


def read_crop(where, same, cross, crop):
    crop[pl.ds(pl.multiple_of(where[2] * 64, 8), 64), :] = same[...]
    crop[pl.ds(pl.multiple_of((1 - where[2]) * 64, 8), 64), :] = cross[...]


def forward_kernel(opening, full, where, *refs):
    if opening:
        state1, state2 = jnp.zeros((128, C1), F32), jnp.zeros((32, C2), F32)
    elif full:
        take_own(where, refs[0:6], (1, 2, 3), None, refs[-1])
        state1, state2 = unfold(refs[-1])
        refs = refs[6:]
    else:
        take(where, refs[0:2], refs[-1])
        state1, state2 = unfold(refs[-1])
        refs = refs[2:]
    same_ref, cross_ref, up_ref, mix_ref, down_ref, aux_ref, out_ref, *rest = refs
    crop_ref, whole = refs[-2:]
    read_crop(where, same_ref, cross_ref, crop_ref)
    if full:
        mixture_ref, slope1_ref, slope2_ref, *slots = rest[:-3]
        factors = rest[-3]
    for column in range(4):
        taps, gain1, gain2 = decode_aux(aux_ref[column])
        narrow = state2.astype(BF16)
        ups = up2(dot(narrow, up_ref[column]))
        mixture = [crop_ref[16 * q : 16 * q + 16, 0:C1] + ups[q] for q in range(8)]
        depth = join(stencil(neighbours(mixture), taps))
        if full:
            active, slope1 = gelu_pair(depth)
        else:
            active = gelu_only(depth)
        hidden = active.astype(BF16)
        state1 = gain1 * state1 + dot(hidden, mix_ref[column])
        pooled = (pool(split(state1)) * 0.25).astype(BF16)
        lifted = dot(pooled, down_ref[column])
        if full:
            active2, slope2 = gelu_pair(lifted)
        else:
            active2 = gelu_only(lifted)
        state2 = gain2 * state2 + active2
        if full:
            mixture_ref[column] = join(mixture)
            slope1_ref[column] = slope1
            slope2_ref[column] = slope2
            put(factors, 0, hidden.astype(F32))
            put(factors, 128, pooled.astype(F32))
            put_two(factors, 160, narrow.astype(F32))
            hand_over(where, column, factors, slots)
    if full:
        put(out_ref, 0, state1)
        put_two(out_ref, 128, state2)
    else:
        give(where, state1, state2, whole, out_ref)


def head_kernel(where, msg_ref, same_ref, cross_ref, one_ref, two_ref, cls_ref, out_ref, first, second, crop_ref):
    read_crop(where, same_ref, cross_ref, crop_ref)
    state1 = msg_ref[0:128, 0:C1].astype(BF16)
    state2 = get_two(msg_ref, 128).astype(BF16)
    labels = crop_ref[:, C1 : C1 + 1].astype(jnp.int32)
    second[...] = dot(state2, two_ref[...])
    first[...] = dot(state1, one_ref[...])
    lateral = first[...] + join(up2(second[...]))
    active, slope = gelu_pair(lateral)
    logits = dot_nt(active.astype(BF16), cls_ref[...])
    classes = lax.broadcasted_iota(jnp.int32, logits.shape, 1)
    logits = logits - jnp.max(logits, axis=-1, keepdims=True)
    powers = jnp.exp(logits)
    probs = powers / jnp.sum(powers, axis=-1, keepdims=True)
    onehot = (classes == labels).astype(F32)
    grad_logits = (probs - onehot) * (loss_scale / 2048.0)
    grad_lat = dot(grad_logits.astype(BF16), cls_ref[...]) * slope
    put(out_ref, 0, dot_nt(grad_lat.astype(BF16), one_ref[...]))
    put_two(out_ref, 128, dot_nt(pool(split(grad_lat)).astype(BF16), two_ref[...]))


def backward_kernel(opening, full, where, *refs):
    if opening:
        head_ref, *refs = refs
        cot1, cot2 = unfold(head_ref)
    elif full:
        take_own(where, refs[0:6], (2, 1, 0), refs[6], refs[-1])
        cot1, cot2 = unfold(refs[-1])
        refs = refs[7:]
    else:
        take(where, refs[0:2], refs[-1])
        cot1, cot2 = unfold(refs[-1])
        refs = refs[2:]
    slope1_ref, slope2_ref, up_ref, mix_ref, down_ref, aux_ref, *rest = refs
    if full:
        mixture_ref, *slots, stem_own, factors, stem_sum, whole = rest
    else:
        out_ref, whole = rest
    for column in (3, 2, 1, 0):
        taps, gain1, gain2 = decode_aux(aux_ref[column])
        grad_s = (cot2 * slope2_ref[column]).astype(BF16)
        back = dot_nt(grad_s, down_ref[column]) * 0.25
        total1 = cot1 + join(up2(back))
        narrow_total = total1.astype(BF16)
        grad_depth = dot_nt(narrow_total, mix_ref[column]) * slope1_ref[column]
        grads = split(grad_depth)
        grad_mixture = stencil(neighbours(grads), taps[::-1])
        grad_narrow = pool(grad_mixture).astype(BF16)
        if not full or column > 0:
            cot2 = gain2 * cot2 + dot_nt(grad_narrow, up_ref[column])
            cot1 = gain1 * total1
        if full:
            put(factors, 0, narrow_total.astype(F32))
            put(factors, 128, grad_narrow.astype(F32))
            put_two(factors, 160, grad_s.astype(F32))
            sums = tap_sums(neighbours(split(mixture_ref[column])), grads)
            put(factors, 224, jnp.concatenate(sums + [jnp.zeros((7, C1), F32)], axis=0))
            hand_over(where, column, factors, slots)
            mixed = join(grad_mixture)
            stem_sum[...] = mixed if column == 3 else stem_sum[...] + mixed
    if full:
        mine = stem_sum[pl.ds(pl.multiple_of(where[2] * 64, 8), 64), :]
        mine = jnp.concatenate([mine, jnp.zeros((64, PAD1 - C1), F32)], axis=1)
        targets = [(where[4 + at], slots[at].at[RROWS // 2 :]) for at in range(3)] + [(where[1], stem_own)]
        for cell in range(4):
            rows = [16 * q + 4 * y + cell for y in range(4) for q in range(4)]
            part = join([mine[row : row + 1] for row in rows])
            for target, ref in targets:

                @pl.when(target == cell)
                def _(part=part, ref=ref):
                    ref[...] = part
    else:
        give(where, cot1, cot2, whole, out_ref)


def weight_kernel(where, lo, l1, l2, l3, m1, m2, m3, ro, r1, r2, r3, s1, s2, s3, stem_own, *rest):
    *outs, c0, c1, c2, c3, left, right = rest
    core = where[2]
    for full_ref, own, pairs, rows in (
        (left, lo, ((l1, m2), (l2, m1), (l3, m3)), LROWS),
        (right, ro, ((r1, s2), (r2, s1), (r3, s3)), RROWS),
    ):
        half = rows // 2
        mine = pl.ds(pl.multiple_of(core * half, 8), half)
        other = pl.ds(pl.multiple_of((1 - core) * half, 8), half)
        full_ref[0] = own[...]
        for at, (near, far) in enumerate(pairs):
            full_ref[at + 1, mine, :] = near[0:half, :]
            full_ref[at + 1, other, :] = far[0:half, :]

    def stack(ref, row, count):
        return jnp.concatenate([ref[q, row : row + count, :] for q in range(4)], axis=0)

    hidden = stack(left, 0, 128)
    pooled = stack(left, 128, 32)
    narrow = jnp.concatenate([stack(left, 160, 32), stack(left, 192, 32)], axis=1)
    total = stack(right, 0, 128).astype(BF16)
    grad_narrow = stack(right, 128, 32).astype(BF16)
    grad_lo = stack(right, 160, 32).astype(BF16)
    grad_hi = stack(right, 192, 32).astype(BF16)
    taps = right[0, 224:240, :] + right[1, 224:240, :] + right[2, 224:240, :] + right[3, 224:240, :]
    for at, out_ref in enumerate(outs):
        block = where[7 + at]
        back1 = lax.rem(PAD1 - 45 * block, PAD1)
        back2 = lax.rem(2 * PAD1 - 90 * block, 2 * PAD1)
        some_hidden = pltpu.roll(hidden, back1, 1)[:, 0:128].astype(BF16)
        some_pooled = pltpu.roll(pooled, back1, 1)[:, 0:128].astype(BF16)
        some_narrow = pltpu.roll(narrow, back2, 1)[:, 0:128].astype(BF16)
        out_ref[0:96, :] = dot_tn(some_narrow, grad_narrow)[0:96]
        out_ref[96:144, :] = dot_tn(some_hidden, total)[0:48]
        out_ref[144:192, :] = dot_tn(some_pooled, grad_lo)[0:48]
        out_ref[192:240, :] = dot_tn(some_pooled, grad_hi)[0:48]
        out_ref[240:256, :] = pltpu.roll(taps, back1, 1)
    z, sign, skip = where[1], 1 - 2 * core, RROWS // 2
    sources = ((stem_own, 0, z), (r1, skip, z - sign), (r2, skip, z + sign), (r3, skip, z + 2))
    for ref, row, source in sources:
        for cell in range(4):
            part = ref[row + 4 * cell : row + 4 * cell + 4, :]
            for shift, out_ref in enumerate((c0, c1, c2, c3)):

                @pl.when(lax.rem(where[0] + shift, 4) == cell)
                def _(part=part, out_ref=out_ref, source=source):
                    out_ref[lax.rem(source + 4, 4)] = part


def final_kernel(where, own, near, far, c0, c1, c2, c3, up_ref, mix_ref, down_ref, tap_ref, stem_ref):
    total = own[...] + near[...] + far[...]
    up_ref[:, 0, :] = total[0:90, 0:C1]
    mix_ref[:, 0, :] = total[96:141, 0:C1]
    down_ref[:, 0, 0:PAD1] = total[144:189]
    down_ref[:, 0, PAD1:C2] = total[192:237, 0 : C2 - PAD1]
    tap_ref[:, 0, :] = total[240:249, 0:45]
    cells = c0[...] + c1[...] + c2[...] + c3[...]
    stem_ref[:, 0] = cells[:, 0:2, 0:C1]
    stem_ref[:, 1] = cells[:, 2:4, 0:C1]


def shape(*dims, kind=F32):
    return jax.ShapeDtypeStruct(dims, kind)


SMEM = pl.BlockSpec(memory_space=pltpu.SMEM)
WHOLE = pl.BlockSpec(memory_space=pltpu.VMEM)
ANY = pl.BlockSpec(memory_space=pl.ANY)
HBM = pl.BlockSpec(memory_space=pltpu.HBM)


def shards(stem, labels, up_proj, mix_proj, down_proj, dw_kernel, gain1, gain2, lat_one, lat_two, classifier):
    y, z = lax.axis_index("y"), lax.axis_index("z")
    core = lax.axis_index("core")
    sign = 1 - 2 * core
    spot = lax.axis_index("xh") * 2 + lax.axis_index("xl")

    def around(at):
        return [(at + sign + 4) % 4, (at - sign + 4) % 4, (at + 2) % 4]

    blocks = [(x % 2) * 4 + core * 2 + x // 2 for x in around(spot) + [spot]]
    where = jnp.stack([y, z, core, spot, *around(z), *blocks]).astype(jnp.int32)

    def z_ring(step):
        return [
            (2 * at + c, 2 * ((at + (step if c == 0 else -step)) % 4) + c) for at in range(4) for c in range(2)
        ]

    def x_spot(x, c):
        return ((x % 2) * 2 + c) * 2 + x // 2

    def x_ring(step):
        return [
            (x_spot(x, c), x_spot((x + (step if c == 0 else -step)) % 4, c)) for x in range(4) for c in range(2)
        ]

    z_axes, x_axes = ("z", "core"), ("xl", "core", "xh")

    def swap(values):
        return lax.ppermute(values, "core", [(0, 1), (1, 0)])

    def deliver(slots):
        near = lax.ppermute(slots[0], z_axes, z_ring(1))
        away = lax.ppermute(slots[1], z_axes, z_ring(-1))
        opposite = lax.ppermute(slots[2], z_axes, z_ring(2))
        return near, away, opposite

    weight_dims = ((C2, C1), (C1, C1), (C1, C2))
    straight, quarter, piece, aux = pl.pallas_call(
        pack_kernel,
        out_shape=(shape(AROWS, 2 * PAD1), shape(QROWS, 2 * PAD1), shape(64, PAD1), shape(8, 2 * PAD1)),
        in_specs=[SMEM] + [HBM] * 8,
        out_specs=(WHOLE,) * 4,
        scratch_shapes=[pltpu.VMEM((1,) + dims, BF16) for dims in weight_dims]
        + [pltpu.VMEM((1, 9, C1), BF16), pltpu.VMEM((1, C1), F32), pltpu.VMEM((1, C2), F32)]
        + [pltpu.VMEM((2, 32, C1), BF16), pltpu.VMEM((2, 32), jnp.int32)]
        + [pltpu.VMEM((WROWS, 2 * PAD1), F32), pltpu.VMEM((3, 2, 32, 128), F32), pltpu.SemaphoreType.DMA((8,))],
        compiler_params=params(PACK_LIMIT),
        name="pack",
    )(where, up_proj, mix_proj, down_proj, dw_kernel, gain1, gain2, stem, labels)

    pairs = [(c, s) for c in range(2) for s in range(2)]
    same = lax.ppermute(piece, ("core", "xh"), [(2 * c + s, 2 * s + c) for c, s in pairs])
    cross = lax.ppermute(piece, ("core", "xh"), [(2 * c + s, 2 * (1 - s) + c) for c, s in pairs])

    def both_ways(values, axes, ring):
        return lax.ppermute(values, axes, ring(1)), lax.ppermute(values, axes, ring(-1))

    near, away = both_ways(quarter, z_axes, z_ring)
    near, away, same, cross = lax.optimization_barrier((near, away, same, cross))
    opposite = lax.ppermute(near, z_axes, z_ring(1))
    opposite, straight = lax.optimization_barrier((opposite, straight))
    quarters = pl.pallas_call(
        join_kernel,
        out_shape=shape(3 * QROWS, 2 * PAD1),
        in_specs=[WHOLE] * 3,
        out_specs=WHOLE,
        compiler_params=params(),
        name="join_quarters",
    )(near, away, opposite)
    straights = both_ways(straight, z_axes, z_ring)
    spread = both_ways(quarters, x_axes, x_ring)
    relays = lax.ppermute(straights[0], z_axes, z_ring(1)), lax.ppermute(spread[0], x_axes, x_ring(1))
    straights, spread, quarters = lax.optimization_barrier((straights, spread, quarters))
    mine = [
        *straights,
        relays[0],
        quarters,
        *spread,
        relays[1],
    ]
    weights = pl.pallas_call(
        columns_kernel,
        out_shape=tuple(shape(4, *dims, kind=BF16) for dims in weight_dims) + (shape(4, 8, 2 * PAD1),),
        in_specs=[SMEM] + [WHOLE] * 14 + [ANY] * 4,
        out_specs=(ANY,) * 4,
        scratch_shapes=[pltpu.VMEM((3,) + dims, BF16) for dims in weight_dims]
        + [pltpu.VMEM((3, 8, 2 * PAD1), F32), pltpu.VMEM((2, WROWS, 2 * PAD1), F32), pltpu.SemaphoreType.DMA((4, 4))],
        compiler_params=params(),
        name="columns",
    )(where, *mine, *[swap(part) for part in mine], up_proj, mix_proj, down_proj, aux)

    whole = pltpu.VMEM((192, PAD1), F32)

    def forward(halves, full):
        dims = [(192, PAD1) if full else (96, PAD1)]
        if full:
            dims += [(4, 128, C1), (4, 128, C1), (4, 32, C2)] + [(LROWS // 2, PAD1)] * 3 + [(LROWS, PAD1)]
        return pl.pallas_call(
            lambda *refs: forward_kernel(not halves, full, *refs),
            out_shape=tuple(shape(*each) for each in dims),
            in_specs=[SMEM] + [WHOLE] * (len(halves) + 6),
            out_specs=(WHOLE,) * len(dims),
            scratch_shapes=[pltpu.VMEM((LROWS, PAD1), F32)] * full + [pltpu.VMEM((128, PAD1), F32), whole],
            compiler_params=params(),
            name="forward_full" if full else "forward_light",
        )(where, *halves, same, cross, *weights)

    def hop(half, pairs):
        half = lax.ppermute(half, "y", pairs)
        return half, swap(half)

    arrived = [()]
    for tick in range(3):
        arrived.append(hop(forward(arrived[-1], False)[0], [(tick, tick + 1)]))
    msg, mixture, slope1, slope2, *lefts, left = forward(sum(arrived, ()), True)
    lefts = deliver(lefts)

    head = pl.pallas_call(
        head_kernel,
        out_shape=shape(192, PAD1),
        in_specs=[SMEM] + [WHOLE] * 6,
        out_specs=WHOLE,
        scratch_shapes=[pltpu.VMEM((128, HEAD), F32), pltpu.VMEM((32, HEAD), F32), pltpu.VMEM((128, PAD1), F32)],
        compiler_params=params(),
        name="head",
    )(where, msg, same, cross, lat_one, lat_two, classifier.T)

    def backward(halves, full):
        operands = [*halves, *([] if halves and not full else [head]), slope1, slope2, *weights]
        dims = [(96, PAD1)]
        if full:
            operands.append(mixture)
            dims = [(RROWS // 2 + 16, PAD1)] * 3 + [(RROWS, PAD1), (16, PAD1)]
        return pl.pallas_call(
            lambda *refs: backward_kernel(not halves, full, *refs),
            out_shape=tuple(shape(*each) for each in dims),
            in_specs=[SMEM] + [WHOLE] * len(operands),
            out_specs=(WHOLE,) * len(dims),
            scratch_shapes=[pltpu.VMEM((RROWS, PAD1), F32), pltpu.VMEM((128, C1), F32)] * full + [whole],
            compiler_params=params(),
            name="backward_full" if full else "backward_light",
        )(where, *operands)

    arrived = [()]
    for tick in range(3):
        arrived.append(hop(backward(arrived[-1], False)[0], [(3 - tick, 2 - tick)]))
        if tick == 1:
            arrived[-1], lefts = lax.optimization_barrier((arrived[-1], lefts))
            mates = [swap(part) for part in lefts]
        if tick == 2:
            arrived[-1], mates = lax.optimization_barrier((arrived[-1], mates))
    slots = backward(sum(arrived, ()), True)
    rights = deliver(slots[0:3])

    *partial, c0, c1, c2, c3 = pl.pallas_call(
        weight_kernel,
        out_shape=(shape(GROWS, PAD1),) * 4 + (shape(4, 4, PAD1),) * 4,
        in_specs=[SMEM] + [WHOLE] * 15,
        out_specs=(WHOLE,) * 8,
        scratch_shapes=[pltpu.VMEM((4, LROWS, PAD1), F32), pltpu.VMEM((4, RROWS, PAD1), F32)],
        compiler_params=params(),
        name="weight_grads",
    )(where, left, *lefts, *mates, slots[3], *rights, *[swap(part) for part in rights], slots[4])
    relay = lax.ppermute(partial[2], x_axes, x_ring(1))
    away = lax.ppermute(partial[1], x_axes, x_ring(-1))
    relay, away, cells = lax.optimization_barrier((relay, away, (c0, c1, c2, c3)))
    passed = pl.pallas_call(
        add_kernel,
        out_shape=shape(GROWS, PAD1),
        in_specs=[WHOLE] * 2,
        out_specs=WHOLE,
        compiler_params=params(),
        name="add_relay",
    )(partial[0], relay)
    near = lax.ppermute(passed, x_axes, x_ring(1))

    def stem_pairs(step):
        return [(4 * at + 2 * k + h, 4 * ((at + step) % 4) + 2 * h + k) for at in range(4) for k, h in pairs]

    cells = [lax.ppermute(cells[step], ("y", "core", "xh"), stem_pairs(step)) for step in range(4)]
    *grads, grad_stem = pl.pallas_call(
        final_kernel,
        out_shape=(shape(90, 1, C1), shape(45, 1, C1), shape(45, 1, C2), shape(9, 1, 45), shape(4, 2, 2, C1)),
        in_specs=[SMEM] + [WHOLE] * 7,
        out_specs=(WHOLE,) * 5,
        compiler_params=params(),
        name="final",
    )(where, partial[3], near, away, *cells)
    return (*[grad.transpose(1, 0, 2) for grad in grads], grad_stem)


def solution(mesh):
    fine = Mesh(mesh.devices.reshape(4, 4, 2, 2, 2), ("y", "z", "xl", "core", "xh"))
    col, dp, strip, both = ("y", "z"), ("xl", "core"), "xh", ("xl", "core", "xh")
    return jax.shard_map(
        shards,
        mesh=fine,
        in_specs=(
            P(dp, strip, None, None),
            P(dp, strip, None),
            P(col, None, None),
            P(col, None, None),
            P(col, None, None),
            P(col, None, None),
            P(col, None),
            P(col, None),
            P(),
            P(),
            P(),
        ),
        out_specs=(
            P(col, both, None),
            P(col, both, None),
            P(col, both, None),
            P(col, None, both),
            P(dp, strip, col, None),
        ),
        check_vma=False,
    )
```
